512 devices in a mesh: grp: 16 (over x_lo, y, core), row: 32 (over z, x_hi).
Axes of the slice: x: 4 (x_hi: 2, x_lo: 2; x = x_hi * 2 + x_lo), y: 4, z: 16, core: 2. Of those that a mesh axis runs over, the one named last changes fastest.
Arguments:
- snapshots: float32 [8192, 8192], P('row', 'grp'), may hold values from -200 to 200
Outputs:
- rotated: float32 [8192, 8192], P('row', 'grp')
The draws below stay inside these ranges and needn't reach their ends.
All inputs are finite; a program needn't handle non-finite values.
Results may differ from the reference program's by a relative error of at most 0.0003.
Values sent between devices are 32-bit elements; how exact they have to be, the bound alone decides.
No kernel may reach another device: no remote copies, remote signals or barrier semaphores. Data moves between devices by JAX's collectives and lax.ppermute only.
A program may use at most 64 MiB of HBM per device.

```python
import math
import jax
import jax.numpy as jnp
import numpy as np
from jax import lax

BLOCK = 256
ROUNDS = 6
NROWS = 8192
COLS = 8192
N_GRP = 16


def draw_snapshots(key, part):
    keys = jax.random.split(jax.random.fold_in(key, 11), 5)
    noise = jnp.clip(jax.random.normal(keys[0], (NROWS, COLS), jnp.float32), -5.0, 5.0)
    col_scale = jnp.exp(jax.random.uniform(keys[2], (1, COLS), jnp.float32, math.log(0.3), math.log(3.0)))
    amplitude = jax.random.uniform(keys[3], (1, COLS), jnp.float32, 0.2, 0.6)
    shared = jnp.clip(jax.random.normal(keys[1], (NROWS, 1), jnp.float32), -4.0, 4.0)
    rising = jnp.exp(0.5 * math.log(3.0) * jnp.arange(NROWS, dtype=jnp.float32)[:, None] / NROWS)
    row_scale = rising * jnp.exp(jax.random.uniform(keys[4], (NROWS, 1), jnp.float32, 0.0, math.log(3.0)))
    values = row_scale * col_scale * (noise + amplitude * shared)
    return values.astype(jnp.float32)


def setup_inputs(seed: int = 0) -> dict:
    splits = jax.random.split(jax.random.key(seed), 2)
    snapshots = draw_snapshots(jax.random.fold_in(splits[1], 71), 0)
    return dict(snapshots=snapshots)


def round_tables(order_size):
    half_order = order_size // 2
    movers = np.arange(1, order_size)
    first_rows = []
    second_rows = []
    for turn_index in range(ROUNDS):
        arranged = np.concatenate([np.zeros(1, np.int64), np.roll(movers, turn_index)])
        first_rows.append(arranged[:half_order])
        second_rows.append(arranged[::-1][:half_order])
    return (jnp.asarray(np.stack(first_rows).astype(np.int32)), jnp.asarray(np.stack(second_rows).astype(np.int32)))

def jacobi_rotation(gram):
    order_size = gram.shape[0]
    first_table, second_table = round_tables(order_size)

    def turn(state_pair, indices):
        matrix, vectors = state_pair
        leading, trailing = indices
        diag_first = matrix[leading, leading]
        diag_second = matrix[trailing, trailing]
        coupling = matrix[leading, trailing]
        difference = diag_second - diag_first
        direction = jnp.where(difference >= 0, 1.0, -1.0)
        denominator = jnp.abs(difference) + jnp.sqrt(difference * difference + 4.0 * coupling * coupling) + 1e-06 * (diag_first + diag_second)
        tangent = direction * 2.0 * coupling / denominator
        cos_part = 1.0 / jnp.sqrt(1.0 + tangent * tangent)
        sine_part = tangent * cos_part

        def mix_columns(array):
            left_cols = array[:, leading]
            right_cols = array[:, trailing]
            array = array.at[:, leading].set(cos_part * left_cols - sine_part * right_cols)
            return array.at[:, trailing].set(sine_part * left_cols + cos_part * right_cols)
        matrix = mix_columns(matrix)
        matrix = mix_columns(matrix.T).T
        vectors = mix_columns(vectors)
        return ((matrix, vectors), None)
    identity = jnp.eye(order_size, dtype=jnp.float32)
    (matrix, vectors), unused = lax.scan(turn, (gram, identity), (first_table, second_table))
    return vectors

def rotate_pair(current):
    gram = jnp.dot(current.T, current, precision=lax.Precision.HIGHEST, preferred_element_type=jnp.float32)
    return jnp.dot(current, jacobi_rotation(gram), precision=lax.Precision.HIGHEST, preferred_element_type=jnp.float32)

def reference(snapshots):
    groups = jnp.transpose(snapshots.reshape(NROWS, N_GRP, 2 * BLOCK), (1, 0, 2))
    turned = lax.map(rotate_pair, groups)
    staying = turned[:, :, :BLOCK]
    arrived = jnp.roll(turned[:, :, BLOCK:], 1, axis=0)
    current = jnp.concatenate([staying, arrived], axis=2)
    finished = lax.map(rotate_pair, current)
    return jnp.transpose(finished, (1, 0, 2)).reshape(NROWS, COLS)
```

```python
import functools

import jax
import jax.numpy as jnp
from jax import lax
from jax.experimental import pallas as pl
from jax.experimental.pallas import tpu as pltpu
from jax.sharding import Mesh
from jax.sharding import PartitionSpec as P

ROUNDS = 6
HALF = 256
REACH = 10
EDGE = 32
DIAGS = 24
MID = 12
LINES = 28

f32 = jnp.float32
INTERPRET = False


def lanes(shape):
    return lax.broadcasted_iota(jnp.int32, shape, 1)


def turn_lanes(x, by):
    by %= x.shape[1]
    return pltpu.roll(x, by, axis=1) if by else x


def turn_lines(x, by):
    return pltpu.roll(x, by % x.shape[0], axis=0)


def mirrored(x):
    n = x.shape[1]
    row = lax.broadcasted_iota(jnp.int32, (n, n), 0)
    flip = jnp.where(row + lanes((n, n)) == n - 1, 1.0, 0.0).astype(jnp.bfloat16)
    high = x.astype(jnp.bfloat16)
    rest = x - high.astype(f32)
    middle = rest.astype(jnp.bfloat16)
    low = (rest - middle.astype(f32)).astype(jnp.bfloat16)
    dot = functools.partial(jnp.dot, preferred_element_type=f32)
    return (dot(low, flip) + dot(middle, flip)) + dot(high, flip)


def ends(t, b):
    t0, t1, b0, b1 = t[:, :128], t[:, 128:], b[:, :128], b[:, 128:]
    at = lanes(t0.shape)
    return jnp.where(
        at < 32, t0, jnp.where(at < 64, turn_lanes(t1, 64), jnp.where(at < 96, turn_lanes(b0, 64), b1))
    )


def band_of(t_ref, b_ref, out_ref):
    count = t_ref.shape[0] // 8

    def same(k, sums):
        at = pl.ds(pl.multiple_of(k * 8, 8), 8)
        t, b = t_ref[at, :], b_ref[at, :]
        new = []
        for j in range(6):
            new.append(sums[j] + t * turn_lanes(t, -2 * j))
        for j in range(6):
            new.append(sums[6 + j] + b * turn_lanes(b, -2 * j))
        return tuple(new)

    def cross(k, sums):
        at = pl.ds(pl.multiple_of(k * 8, 8), 8)
        t, b = t_ref[at, :], b_ref[at, :]
        new = []
        for j in range(6):
            new.append(sums[j] + t * turn_lanes(b, -2 * j))
        for j in range(1, 6):
            new.append(sums[5 + j] + b * turn_lanes(t, -2 * j))
        e = ends(t, b)
        swapped = turn_lanes(e, 64)
        for j in range(5):
            new.append(sums[11 + j] + e * turn_lanes(e, -2 * j - 1))
        for j in range(5):
            new.append(sums[16 + j] + e * turn_lanes(swapped, -2 * j - 1))
        return tuple(new)

    wide, narrow = jnp.zeros((8, 256), f32), jnp.zeros((8, 128), f32)
    first = lax.fori_loop(0, count, same, (wide,) * 12)
    second = lax.fori_loop(0, count, cross, (wide,) * 11 + (narrow,) * 10)

    def put(line, value):
        for k in range(out_ref.shape[0]):
            out_ref[k, line : line + 1, :] = value

    for line, value in enumerate(first + second[:11]):
        total = jnp.sum(value, axis=0, keepdims=True)
        put(line, total[:, :128])
        put(LINES + line, total[:, 128:])
    for j in range(5):
        put(23 + j, jnp.sum(second[11 + j], axis=0, keepdims=True))
        put(LINES + 23 + j, jnp.sum(second[16 + j], axis=0, keepdims=True))


def spread(e, top):
    both = jnp.concatenate([e, e], axis=1)
    at = lanes(both.shape)
    first, last = (both, turn_lanes(both, 64)) if top else (turn_lanes(both, -64), both)
    return jnp.where(at < EDGE, first, jnp.where(at >= HALF - EDGE, last, 0.0))


def along_columns(x):
    shifted = jnp.broadcast_to(turn_lanes(x, -MID), (DIAGS, HALF))
    return pltpu.roll(shifted, 0, axis=1, stride=1, stride_axis=0)


def angles_of(parts_ref, x_ref):
    band = parts_ref[0]
    for k in range(1, parts_ref.shape[0]):
        band = band + parts_ref[k]
    low, high = band[:LINES], band[LINES:]
    blank = jnp.zeros((1, HALF), f32)
    for block in range(4):
        for line in (0, DIAGS - 2, DIAGS - 1):
            x_ref[block, line : line + 1, :] = blank
    TT, TB, BT, BB = 0, 1, 2, 3

    def put(block, other, d, value):
        x_ref[block, MID - d : MID - d + 1, :] = value
        x_ref[other, MID + d : MID + d + 1, :] = turn_lanes(value, d)

    def line(k):
        return jnp.concatenate([low[k : k + 1], high[k : k + 1]], axis=1)

    for j in range(6):
        put(TT, TT, 2 * j, line(j))
        put(BB, BB, 2 * j, line(6 + j))
        put(TB, BT, 2 * j, line(12 + j))
        if j:
            put(BT, TB, 2 * j, line(17 + j))
    alike, across = low[23:28], high[23:28]
    odd = [
        (TT, TT, spread(alike, True)),
        (BB, BB, spread(alike, False)),
        (TB, BT, spread(across, True)),
        (BT, TB, spread(across, False)),
    ]
    for block, other, value in odd:
        for j in range(5):
            put(block, other, 2 * j + 1, value[j : j + 1])

    tt, tb, bt, bb = (x_ref[k] for k in range(4))
    shape = (DIAGS, HALF)
    i = lanes(shape)
    j = i + MID - lax.broadcasted_iota(jnp.int32, shape, 0)
    i_one, i_more, i_last = i == 1, i >= 2, i == HALF - 1
    j_one, j_more, j_last = j == 1, j >= 2, j == HALF - 1

    def less(x):
        return turn_lines(x, -1)

    def more(x):
        return turn_lines(x, 1)

    cosines, sines = [], []
    for turn in range(ROUNDS):
        first, second, coupling = (x[MID : MID + 1] for x in (tt, bb, tb))
        difference = second - first
        direction = jnp.where(difference >= 0, 1.0, -1.0)
        denominator = (
            jnp.abs(difference)
            + jnp.sqrt(difference * difference + 4.0 * coupling * coupling)
            + 1e-06 * (first + second)
        )
        tangent = direction * 2.0 * coupling / denominator
        c = 1.0 / jnp.sqrt(1.0 + tangent * tangent)
        s = tangent * c
        cosines.append(c)
        sines.append(s)
        if turn == ROUNDS - 1:
            break
        c_row, s_row = jnp.broadcast_to(c, shape), jnp.broadcast_to(s, shape)
        c_col, s_col = along_columns(c), along_columns(s)
        tt, tb = c_col * tt - s_col * tb, s_col * tt + c_col * tb
        bt, bb = c_col * bt - s_col * bb, s_col * bt + c_col * bb
        tt, bt = c_row * tt - s_row * bt, s_row * tt + c_row * bt
        tb, bb = c_row * tb - s_row * bb, s_row * tb + c_row * bb
        tt, tb = (
            jnp.where(j_more, less(tt), jnp.where(j_one, less(tb), tt)),
            jnp.where(j_last, tt, more(tb)),
        )
        bt, bb = (
            jnp.where(j_more, less(bt), jnp.where(j_one, less(bb), bt)),
            jnp.where(j_last, bt, more(bb)),
        )
        tt, bt = (
            jnp.where(i_more, turn_lanes(more(tt), 1), jnp.where(i_one, turn_lanes(more(bt), 1), tt)),
            jnp.where(i_last, tt, turn_lanes(less(bt), -1)),
        )
        tb, bb = (
            jnp.where(i_more, turn_lanes(more(tb), 1), jnp.where(i_one, turn_lanes(more(bb), 1), tb)),
            jnp.where(i_last, tb, turn_lanes(less(bb), -1)),
        )
    return cosines, sines


def turned(t, b, cosines, sines):
    at = lanes(t.shape)
    none, one, more, last = at == 0, at == 1, at >= 2, at == HALF - 1
    for turn in range(ROUNDS):
        c, s = cosines[turn], sines[turn]
        t, b = c * t - s * b, s * t + c * b
        if turn < ROUNDS - 1:
            t, b = (
                jnp.where(more, turn_lanes(t, 1), jnp.where(one, turn_lanes(b, 1), t)),
                jnp.where(last, t, turn_lanes(b, -1)),
            )
    for turn in range(ROUNDS - 1):
        t, b = (
            jnp.where(none, t, jnp.where(last, b, turn_lanes(t, -1))),
            jnp.where(none, turn_lanes(t, -1), turn_lanes(b, 1)),
        )
    return t, b


def each_chunk(t_ref, b_ref, t_out, b_out, cosines, sines, rows=16):
    shape = (rows, HALF)
    cosines = [jnp.broadcast_to(c, shape) for c in cosines]
    sines = [jnp.broadcast_to(s, shape) for s in sines]

    def chunk(k, carry):
        at = pl.ds(pl.multiple_of(k * rows, rows), rows)
        t_out[at, :], b_out[at, :] = turned(t_ref[at, :], b_ref[at, :], cosines, sines)
        return carry

    lax.fori_loop(0, t_ref.shape[0] // rows, chunk, 0)


def first_band(p_ref, out_ref, b_ref):
    b_ref[...] = mirrored(p_ref[:, HALF:])
    band_of(p_ref.at[:, :HALF], b_ref, out_ref)


def first_turn(parts_ref, p_ref, b_ref, t_out, b_out, x_ref):
    cosines, sines = angles_of(parts_ref, x_ref)
    each_chunk(p_ref.at[:, :HALF], b_ref, t_out, b_out, cosines, sines)


def second_band(t_ref, b_ref, out_ref):
    band_of(t_ref, b_ref, out_ref)


def second_turn(parts_ref, t_ref, b_ref, out_ref, x_ref, b_out):
    cosines, sines = angles_of(parts_ref, x_ref)
    each_chunk(t_ref, b_ref, out_ref.at[:, :HALF], b_out, cosines, sines)
    out_ref[:, HALF:] = mirrored(b_out[...])


def call(body, outs, args, scratch=()):
    vmem = pl.BlockSpec(memory_space=pltpu.VMEM)
    shapes = [jax.ShapeDtypeStruct(s, f32) for s in outs]
    return pl.pallas_call(
        body,
        out_shape=shapes,
        in_specs=[vmem] * len(args),
        out_specs=[vmem] * len(outs),
        scratch_shapes=[pltpu.VMEM(s, f32) for s in scratch],
        compiler_params=pltpu.CompilerParams(vmem_limit_bytes=32 * 1024 * 1024),
        interpret=INTERPRET,
    )(*args)


NEAR, FAR = ("near",), ("far", "side")


def exchanged(parts, near, far):
    arrived = lax.all_to_all(parts, NEAR, 0, 0, tiled=True)
    total = arrived[0]
    for k in range(1, near):
        total = total + arrived[k]
    again = jnp.broadcast_to(total[None], (far, *total.shape))
    return lax.all_to_all(again, FAR, 0, 0, tiled=True)


def per_device(snapshots, near, far, groups):
    rows = snapshots.shape[0]
    square, band, state = (rows, HALF), (near, 2 * LINES, 128), (4, DIAGS, HALF)
    parts, b = call(first_band, [band, square], [snapshots])
    t, b = call(first_turn, [square, square], [exchanged(parts, near, far), snapshots, b], [state])
    b = lax.ppermute(b, "grp", [(i, (i + 1) % groups) for i in range(groups)])
    (parts,) = call(second_band, [band], [t, b])
    (out,) = call(
        second_turn, [(rows, 2 * HALF)], [exchanged(parts, near, far), t, b], [state, square]
    )
    return out


def solution(mesh):
    groups, rows = mesh.shape["grp"], mesh.shape["row"]
    near, side = 4, 2
    far = rows // (near * side)
    fine = Mesh(mesh.devices.reshape(groups, far, near, side), ("grp", "far", "near", "side"))
    placed = P(("far", "near", "side"), "grp")
    body = functools.partial(per_device, near=near, far=far * side, groups=groups)
    return jax.shard_map(body, mesh=fine, in_specs=(placed,), out_specs=placed, check_vma=False)
```

```python
import functools

import jax
import jax.numpy as jnp
from jax import lax
from jax.experimental import pallas as pl
from jax.experimental.pallas import tpu as pltpu
from jax.sharding import Mesh
from jax.sharding import PartitionSpec as P

ROUNDS = 6
HALF = 256
REACH = 10
EDGE = 32
DIAGS = 24
MID = 12
LINES = 56

f32 = jnp.float32
INTERPRET = False


def lanes(shape):
    return lax.broadcasted_iota(jnp.int32, shape, 1)


def turn_lanes(x, by):
    by %= x.shape[1]
    return pltpu.roll(x, by, axis=1) if by else x


def turn_lines(x, by):
    return pltpu.roll(x, by % x.shape[0], axis=0)


def picked(x, index):
    return jnp.take_along_axis(x, index, axis=1, mode="promise_in_bounds")


def mirrored(low, high):
    index = 127 - lanes(low.shape)
    return picked(high, index), picked(low, index)


def ends(t, b):
    at = lanes(t[0].shape)
    return jnp.where(
        at < 32, t[0], jnp.where(at < 64, turn_lanes(t[1], 64), jnp.where(at < 96, turn_lanes(b[0], 64), b[1]))
    )


def ahead(x, d):
    low, high = (turn_lanes(half, -d) for half in x)
    return jnp.where(lanes(low.shape) < 128 - d, low, high), high


def halves(ref, at):
    return ref[at, :128], ref[at, 128:256]


def band_of(load, count, out_ref, sums_ref):
    def over_rows(step, n, width):
        zeros = tuple(jnp.zeros((8, 128), f32) for _ in range(n * width))
        return lax.fori_loop(0, count, lambda k, sums: step(*load(k), sums), zeros, unroll=4)

    def with_top(t, b, sums):
        new = []
        for d in range(0, REACH + 1, 2):
            shifted = ahead(t, d) if d else t
            for left in (t, b) if d else (t,):
                new += [left[h] * shifted[h] for h in range(2)]
        return tuple(x + y for x, y in zip(sums, new))

    def with_bottom(t, b, sums):
        new = []
        for d in range(0, REACH + 1, 2):
            shifted = ahead(b, d) if d else b
            for left in (b, t):
                new += [left[h] * shifted[h] for h in range(2)]
        return tuple(x + y for x, y in zip(sums, new))

    def at_ends(t, b, sums):
        e = ends(t, b)
        swapped = turn_lanes(e, 64)
        new = [e * turn_lanes(e, -d) for d in range(1, REACH, 2)]
        new += [e * turn_lanes(swapped, -d) for d in range(1, REACH, 2)]
        return tuple(x + y for x, y in zip(sums, new))

    def keep(line, value):
        sums_ref[pl.ds(8 * line, 8), :] = value

    sums = over_rows(with_top, 11, 2)
    for h in range(2):
        keep(24 * h, sums[h])
        for j in range(1, 6):
            keep(24 * h + j, sums[4 * j - 2 + h])
            keep(24 * h + 17 + j, sums[4 * j + h])
    sums = over_rows(with_bottom, 12, 2)
    for h in range(2):
        for j in range(6):
            keep(24 * h + 6 + j, sums[4 * j + h])
            keep(24 * h + 12 + j, sums[4 * j + 2 + h])
    sums = over_rows(at_ends, 10, 1)
    for line, j in enumerate((0, 1, 2, 3, 5, 6, 7, 8)):
        keep(48 + line, sums[j])
    keep(23, sums[4])
    keep(47, sums[9])
    parts = [sums_ref[pl.ds(k, LINES, stride=8), :] for k in range(8)]
    while len(parts) > 1:
        parts = [x + y for x, y in zip(parts[::2], parts[1::2])]
    for k in range(out_ref.shape[0]):
        out_ref[k] = parts[0]


def spread(e, top):
    both = jnp.concatenate([e, e], axis=1)
    at = lanes(both.shape)
    first, last = (both, turn_lanes(both, 64)) if top else (turn_lanes(both, -64), both)
    return jnp.where(at < EDGE, first, jnp.where(at >= HALF - EDGE, last, 0.0))


def along_columns(x):
    shifted = jnp.broadcast_to(turn_lanes(x, -MID), (DIAGS, HALF))
    return pltpu.roll(shifted, 0, axis=1, stride=1, stride_axis=0)


def angles_of(parts_ref, x_ref):
    band = parts_ref[0]
    for k in range(1, parts_ref.shape[0]):
        band = band + parts_ref[k]
    low, high, narrow = band[:24], band[24:48], band[48:56]
    blank = jnp.zeros((1, HALF), f32)
    for block in range(4):
        for line in (0, DIAGS - 2, DIAGS - 1):
            x_ref[block, line : line + 1, :] = blank
    TT, TB, BT, BB = 0, 1, 2, 3

    def put(block, other, d, value):
        x_ref[block, MID - d : MID - d + 1, :] = value
        x_ref[other, MID + d : MID + d + 1, :] = turn_lanes(value, d)

    def line(k):
        return jnp.concatenate([low[k : k + 1], high[k : k + 1]], axis=1)

    for j in range(6):
        put(TT, TT, 2 * j, line(j))
        put(BB, BB, 2 * j, line(6 + j))
        put(TB, BT, 2 * j, line(12 + j))
        if j:
            put(BT, TB, 2 * j, line(17 + j))
    alike = jnp.concatenate([narrow[:4], low[23:24]], axis=0)
    across = jnp.concatenate([narrow[4:], high[23:24]], axis=0)
    odd = [
        (TT, TT, spread(alike, True)),
        (BB, BB, spread(alike, False)),
        (TB, BT, spread(across, True)),
        (BT, TB, spread(across, False)),
    ]
    for block, other, value in odd:
        for j in range(5):
            put(block, other, 2 * j + 1, value[j : j + 1])

    tt, tb, bt, bb = (x_ref[k] for k in range(4))
    shape = (DIAGS, HALF)
    i = lanes(shape)
    j = i + MID - lax.broadcasted_iota(jnp.int32, shape, 0)
    i_one, i_more, i_last = i == 1, i >= 2, i == HALF - 1
    j_one, j_more, j_last = j == 1, j >= 2, j == HALF - 1

    def less(x):
        return turn_lines(x, -1)

    def more(x):
        return turn_lines(x, 1)

    cosines, sines = [], []
    for turn in range(ROUNDS):
        first, second, coupling = (x[MID : MID + 1] for x in (tt, bb, tb))
        difference = second - first
        direction = jnp.where(difference >= 0, 1.0, -1.0)
        denominator = (
            jnp.abs(difference)
            + jnp.sqrt(difference * difference + 4.0 * coupling * coupling)
            + 1e-06 * (first + second)
        )
        tangent = direction * 2.0 * coupling / denominator
        c = 1.0 / jnp.sqrt(1.0 + tangent * tangent)
        s = tangent * c
        cosines.append(c)
        sines.append(s)
        if turn == ROUNDS - 1:
            break
        c_row, s_row = jnp.broadcast_to(c, shape), jnp.broadcast_to(s, shape)
        c_col, s_col = along_columns(c), along_columns(s)
        tt, tb = c_col * tt - s_col * tb, s_col * tt + c_col * tb
        bt, bb = c_col * bt - s_col * bb, s_col * bt + c_col * bb
        tt, bt = c_row * tt - s_row * bt, s_row * tt + c_row * bt
        tb, bb = c_row * tb - s_row * bb, s_row * tb + c_row * bb
        tt, tb = (
            jnp.where(j_more, less(tt), jnp.where(j_one, less(tb), tt)),
            jnp.where(j_last, tt, more(tb)),
        )
        bt, bb = (
            jnp.where(j_more, less(bt), jnp.where(j_one, less(bb), bt)),
            jnp.where(j_last, bt, more(bb)),
        )
        tt, bt = (
            jnp.where(i_more, turn_lanes(more(tt), 1), jnp.where(i_one, turn_lanes(more(bt), 1), tt)),
            jnp.where(i_last, tt, turn_lanes(less(bt), -1)),
        )
        tb, bb = (
            jnp.where(i_more, turn_lanes(more(tb), 1), jnp.where(i_one, turn_lanes(more(bb), 1), tb)),
            jnp.where(i_last, tb, turn_lanes(less(bb), -1)),
        )
    return cosines, sines


def advanced(t, b):
    at = lanes(t[0].shape)
    t0, t1, b0, b1 = turn_lanes(t[0], 1), turn_lanes(t[1], 1), turn_lanes(b[0], -1), turn_lanes(b[1], -1)
    return (
        (
            jnp.where(at >= 2, t0, jnp.where(at == 1, turn_lanes(b[0], 1), t[0])),
            jnp.where(at >= 1, t1, t0),
        ),
        (jnp.where(at == 127, b1, b0), jnp.where(at == 127, t[1], b1)),
    )


MOVES = ROUNDS - 1


def retreated_top(t, b):
    at = lanes(t[0].shape)
    back = [turn_lanes(x, -MOVES) for x in t]
    from_bottom = picked(b[1], (250 - at) % 128)
    return (
        jnp.where(at == 0, t[0], jnp.where(at < 128 - MOVES, back[0], back[1])),
        jnp.where(at < 128 - MOVES, back[1], from_bottom),
    )


def retreated_bottom(t, b):
    at = lanes(t[0].shape)
    on = [turn_lanes(x, MOVES) for x in b]
    from_top = picked(t[0], (MOVES - at) % 128)
    return (
        jnp.where(at < MOVES, from_top, on[0]),
        jnp.where(at < MOVES, on[0], on[1]),
    )


def unfolded_bottom(t, b):
    at = lanes(t[0].shape)
    index = (122 - at) % 128
    low, high = picked(b[0], index), picked(b[1], index)
    return (
        jnp.where(at <= 122, high, low),
        jnp.where(at <= 122, low, turn_lanes(t[0], 122)),
    )


def turned_chunks(load, store, count, rows, cosines, sines):
    def chunk(k, carry):
        t, b = load(k)
        for turn in range(ROUNDS):
            c, s = cosines[turn], sines[turn]
            t, b = (
                tuple(c[h] * t[h] - s[h] * b[h] for h in range(2)),
                tuple(s[h] * t[h] + c[h] * b[h] for h in range(2)),
            )
            if turn < MOVES:
                t, b = advanced(t, b)
        store(k, t, b)
        return carry

    def wide(x):
        x = jnp.broadcast_to(x, (rows, HALF))
        return x[:, :128], x[:, 128:]

    cosines, sines = [wide(c) for c in cosines], [wide(s) for s in sines]
    lax.fori_loop(0, count, chunk, 0)


def rows_at(k, rows):
    return pl.ds(pl.multiple_of(k * rows, rows), rows)


CHUNK = 32


def first_band(p_ref, out_ref, b_ref, sums_ref):
    def fold(k, carry):
        at = rows_at(k, CHUNK)
        b_ref[at, :128], b_ref[at, 128:] = mirrored(p_ref[at, 256:384], p_ref[at, 384:])
        return carry

    lax.fori_loop(0, p_ref.shape[0] // CHUNK, fold, 0)

    def load(k):
        at = rows_at(k, 8)
        return halves(p_ref, at), halves(b_ref, at)

    band_of(load, p_ref.shape[0] // 8, out_ref, sums_ref)


def second_band(t_ref, b_ref, out_ref, sums_ref):
    def load(k):
        at = rows_at(k, 8)
        return halves(t_ref, at), halves(b_ref, at)

    band_of(load, t_ref.shape[0] // 8, out_ref, sums_ref)


def first_turn(parts_ref, t_ref, b_ref, t_out, b_out, x_ref):
    cosines, sines = angles_of(parts_ref, x_ref)

    def load(k):
        at = rows_at(k, CHUNK)
        return halves(t_ref, at), halves(b_ref, at)

    def store(k, t, b):
        at = rows_at(k, CHUNK)
        t_out[at, :128], t_out[at, 128:] = retreated_top(t, b)
        b_out[at, :128], b_out[at, 128:] = retreated_bottom(t, b)

    turned_chunks(load, store, t_ref.shape[0] // CHUNK, CHUNK, cosines, sines)


def second_turn(parts_ref, t_ref, b_ref, out_ref, x_ref):
    cosines, sines = angles_of(parts_ref, x_ref)

    def load(k):
        at = rows_at(k, CHUNK)
        return halves(t_ref, at), halves(b_ref, at)

    def store(k, t, b):
        at = rows_at(k, CHUNK)
        out_ref[at, :128], out_ref[at, 128:256] = retreated_top(t, b)
        out_ref[at, 256:384], out_ref[at, 384:] = unfolded_bottom(t, b)

    turned_chunks(load, store, t_ref.shape[0] // CHUNK, CHUNK, cosines, sines)


def call(body, outs, args, scratch=()):
    vmem = pl.BlockSpec(memory_space=pltpu.VMEM)
    shapes = [jax.ShapeDtypeStruct(s, f32) for s in outs]
    return pl.pallas_call(
        body,
        out_shape=shapes,
        in_specs=[vmem] * len(args),
        out_specs=[vmem] * len(outs),
        scratch_shapes=[pltpu.VMEM(s, f32) for s in scratch],
        compiler_params=pltpu.CompilerParams(vmem_limit_bytes=32 * 1024 * 1024),
        interpret=INTERPRET,
    )(*args)


NEAR, FAR = ("near",), ("far", "side")


def exchanged(parts, near, far):
    arrived = lax.all_to_all(parts, NEAR, 0, 0, tiled=True)
    total = arrived[0]
    for k in range(1, near):
        total = total + arrived[k]
    again = jnp.broadcast_to(total[None], (far, *total.shape))
    return lax.all_to_all(again, FAR, 0, 0, tiled=True)


SUMS = [(8 * LINES, 128)]
STATE = [(4, DIAGS, HALF)]


def per_device(snapshots, near, far, groups):
    rows = snapshots.shape[0]
    square, band = (rows, HALF), (near, LINES, 128)
    parts, b = call(first_band, [band, square], [snapshots], SUMS)
    t, b = call(first_turn, [square, square], [exchanged(parts, near, far), snapshots, b], STATE)
    b = lax.ppermute(b, "grp", [(i, (i + 1) % groups) for i in range(groups)])
    (parts,) = call(second_band, [band], [t, b], SUMS)
    (out,) = call(second_turn, [(rows, 2 * HALF)], [exchanged(parts, near, far), t, b], STATE)
    return out


def solution(mesh):
    groups, rows = mesh.shape["grp"], mesh.shape["row"]
    near, side = 4, 2
    far = rows // (near * side)
    fine = Mesh(mesh.devices.reshape(groups, far, near, side), ("grp", "far", "near", "side"))
    placed = P(("far", "near", "side"), "grp")
    body = functools.partial(per_device, near=near, far=far * side, groups=groups)
    return jax.shard_map(body, mesh=fine, in_specs=(placed,), out_specs=placed, check_vma=False)
```

```python
import functools

import jax
import jax.numpy as jnp
from jax import lax
from jax.experimental import pallas as pl
from jax.experimental.pallas import tpu as pltpu
from jax.sharding import Mesh
from jax.sharding import PartitionSpec as P

ROUNDS = 6
HALF = 256
REACH = 10
EDGE = 32
DIAGS = 24
MID = 12
LINES = 56

f32 = jnp.float32
INTERPRET = False


def lanes(shape):
    return lax.broadcasted_iota(jnp.int32, shape, 1)


def turn_lanes(x, by):
    by %= x.shape[1]
    return pltpu.roll(x, by, axis=1) if by else x


def turn_lines(x, by):
    return pltpu.roll(x, by % x.shape[0], axis=0)


def picked(x, index):
    return jnp.take_along_axis(x, index, axis=1, mode="promise_in_bounds")


def mirrored(low, high):
    index = 127 - lanes(low.shape)
    return picked(high, index), picked(low, index)


def ends(t, b):
    at = lanes(t[0].shape)
    return jnp.where(
        at < 32, t[0], jnp.where(at < 64, turn_lanes(t[1], 64), jnp.where(at < 96, turn_lanes(b[0], 64), b[1]))
    )


def ahead(x, d):
    low, high = (turn_lanes(half, -d) for half in x)
    return jnp.where(lanes(low.shape) < 128 - d, low, high), high


def halves(ref, at):
    return ref[at, :128], ref[at, 128:256]


def band_of(load, count, out_ref, sums_ref):
    def over_rows(step, n, width):
        zeros = tuple(jnp.zeros((8, 128), f32) for _ in range(n * width))
        return lax.fori_loop(0, count, lambda k, sums: step(*load(k), sums), zeros, unroll=16)

    def with_top(t, b, sums):
        new = []
        for d in range(0, REACH + 1, 2):
            shifted = ahead(t, d) if d else t
            for left in (t, b) if d else (t,):
                new += [left[h] * shifted[h] for h in range(2)]
        return tuple(x + y for x, y in zip(sums, new))

    def with_bottom(t, b, sums):
        new = []
        for d in range(0, REACH + 1, 2):
            shifted = ahead(b, d) if d else b
            for left in (b, t):
                new += [left[h] * shifted[h] for h in range(2)]
        return tuple(x + y for x, y in zip(sums, new))

    def at_ends(t, b, sums):
        e = ends(t, b)
        swapped = turn_lanes(e, 64)
        new = [e * turn_lanes(e, -d) for d in range(1, REACH, 2)]
        new += [e * turn_lanes(swapped, -d) for d in range(1, REACH, 2)]
        return tuple(x + y for x, y in zip(sums, new))

    def keep(line, value):
        sums_ref[pl.ds(8 * line, 8), :] = value

    sums = over_rows(with_top, 11, 2)
    for h in range(2):
        keep(24 * h, sums[h])
        for j in range(1, 6):
            keep(24 * h + j, sums[4 * j - 2 + h])
            keep(24 * h + 17 + j, sums[4 * j + h])
    sums = over_rows(with_bottom, 12, 2)
    for h in range(2):
        for j in range(6):
            keep(24 * h + 6 + j, sums[4 * j + h])
            keep(24 * h + 12 + j, sums[4 * j + 2 + h])
    sums = over_rows(at_ends, 10, 1)
    for line, j in enumerate((0, 1, 2, 3, 5, 6, 7, 8)):
        keep(48 + line, sums[j])
    keep(23, sums[4])
    keep(47, sums[9])
    parts = [sums_ref[pl.ds(k, LINES, stride=8), :] for k in range(8)]
    while len(parts) > 1:
        parts = [x + y for x, y in zip(parts[::2], parts[1::2])]
    for k in range(out_ref.shape[0]):
        out_ref[k] = parts[0]


def spread(e, top):
    both = jnp.concatenate([e, e], axis=1)
    at = lanes(both.shape)
    first, last = (both, turn_lanes(both, 64)) if top else (turn_lanes(both, -64), both)
    return jnp.where(at < EDGE, first, jnp.where(at >= HALF - EDGE, last, 0.0))


def along_columns(x):
    shifted = jnp.broadcast_to(turn_lanes(x, -MID), (DIAGS, HALF))
    return pltpu.roll(shifted, 0, axis=1, stride=1, stride_axis=0)


def angles_of(parts_ref, x_ref):
    band = parts_ref[0]
    for k in range(1, parts_ref.shape[0]):
        band = band + parts_ref[k]
    low, high, narrow = band[:24], band[24:48], band[48:56]
    blank = jnp.zeros((1, HALF), f32)
    for block in range(4):
        for line in (0, DIAGS - 2, DIAGS - 1):
            x_ref[block, line : line + 1, :] = blank
    TT, TB, BT, BB = 0, 1, 2, 3

    def put(block, other, d, value):
        x_ref[block, MID - d : MID - d + 1, :] = value
        x_ref[other, MID + d : MID + d + 1, :] = turn_lanes(value, d)

    def line(k):
        return jnp.concatenate([low[k : k + 1], high[k : k + 1]], axis=1)

    for j in range(6):
        put(TT, TT, 2 * j, line(j))
        put(BB, BB, 2 * j, line(6 + j))
        put(TB, BT, 2 * j, line(12 + j))
        if j:
            put(BT, TB, 2 * j, line(17 + j))
    alike = jnp.concatenate([narrow[:4], low[23:24]], axis=0)
    across = jnp.concatenate([narrow[4:], high[23:24]], axis=0)
    odd = [
        (TT, TT, spread(alike, True)),
        (BB, BB, spread(alike, False)),
        (TB, BT, spread(across, True)),
        (BT, TB, spread(across, False)),
    ]
    for block, other, value in odd:
        for j in range(5):
            put(block, other, 2 * j + 1, value[j : j + 1])

    tt, tb, bt, bb = (x_ref[k] for k in range(4))
    shape = (DIAGS, HALF)
    i = lanes(shape)
    j = i + MID - lax.broadcasted_iota(jnp.int32, shape, 0)
    i_one, i_more, i_last = i == 1, i >= 2, i == HALF - 1
    j_one, j_more, j_last = j == 1, j >= 2, j == HALF - 1

    def less(x):
        return turn_lines(x, -1)

    def more(x):
        return turn_lines(x, 1)

    cosines, sines = [], []
    for turn in range(ROUNDS):
        first, second, coupling = (x[MID : MID + 1] for x in (tt, bb, tb))
        difference = second - first
        direction = jnp.where(difference >= 0, 1.0, -1.0)
        denominator = (
            jnp.abs(difference)
            + jnp.sqrt(difference * difference + 4.0 * coupling * coupling)
            + 1e-06 * (first + second)
        )
        tangent = direction * 2.0 * coupling / denominator
        c = 1.0 / jnp.sqrt(1.0 + tangent * tangent)
        s = tangent * c
        cosines.append(c)
        sines.append(s)
        if turn == ROUNDS - 1:
            break
        c_row, s_row = jnp.broadcast_to(c, shape), jnp.broadcast_to(s, shape)
        c_col, s_col = along_columns(c), along_columns(s)
        tt, tb = c_col * tt - s_col * tb, s_col * tt + c_col * tb
        bt, bb = c_col * bt - s_col * bb, s_col * bt + c_col * bb
        tt, bt = c_row * tt - s_row * bt, s_row * tt + c_row * bt
        tb, bb = c_row * tb - s_row * bb, s_row * tb + c_row * bb
        tt, tb = (
            jnp.where(j_more, less(tt), jnp.where(j_one, less(tb), tt)),
            jnp.where(j_last, tt, more(tb)),
        )
        bt, bb = (
            jnp.where(j_more, less(bt), jnp.where(j_one, less(bb), bt)),
            jnp.where(j_last, bt, more(bb)),
        )
        tt, bt = (
            jnp.where(i_more, turn_lanes(more(tt), 1), jnp.where(i_one, turn_lanes(more(bt), 1), tt)),
            jnp.where(i_last, tt, turn_lanes(less(bt), -1)),
        )
        tb, bb = (
            jnp.where(i_more, turn_lanes(more(tb), 1), jnp.where(i_one, turn_lanes(more(bb), 1), tb)),
            jnp.where(i_last, tb, turn_lanes(less(bb), -1)),
        )
    return cosines, sines


def advanced(t, b):
    at = lanes(t[0].shape)
    t0, t1, b0, b1 = turn_lanes(t[0], 1), turn_lanes(t[1], 1), turn_lanes(b[0], -1), turn_lanes(b[1], -1)
    return (
        (
            jnp.where(at >= 2, t0, jnp.where(at == 1, turn_lanes(b[0], 1), t[0])),
            jnp.where(at >= 1, t1, t0),
        ),
        (jnp.where(at == 127, b1, b0), jnp.where(at == 127, t[1], b1)),
    )


MOVES = ROUNDS - 1


def retreated_top(t, b):
    at = lanes(t[0].shape)
    back = [turn_lanes(x, -MOVES) for x in t]
    from_bottom = picked(b[1], (250 - at) % 128)
    return (
        jnp.where(at == 0, t[0], jnp.where(at < 128 - MOVES, back[0], back[1])),
        jnp.where(at < 128 - MOVES, back[1], from_bottom),
    )


def retreated_bottom(t, b):
    at = lanes(t[0].shape)
    on = [turn_lanes(x, MOVES) for x in b]
    from_top = picked(t[0], (MOVES - at) % 128)
    return (
        jnp.where(at < MOVES, from_top, on[0]),
        jnp.where(at < MOVES, on[0], on[1]),
    )


def unfolded_bottom(t, b):
    at = lanes(t[0].shape)
    index = (122 - at) % 128
    low, high = picked(b[0], index), picked(b[1], index)
    return (
        jnp.where(at <= 122, high, low),
        jnp.where(at <= 122, low, turn_lanes(t[0], 122)),
    )


def turned_chunks(load, store, count, rows, cosines, sines):
    def chunk(k, carry):
        t, b = load(k)
        for turn in range(ROUNDS):
            c, s = cosines[turn], sines[turn]
            t, b = (
                tuple(c[h] * t[h] - s[h] * b[h] for h in range(2)),
                tuple(s[h] * t[h] + c[h] * b[h] for h in range(2)),
            )
            if turn < MOVES:
                t, b = advanced(t, b)
        store(k, t, b)
        return carry

    def wide(x):
        x = jnp.broadcast_to(x, (rows, HALF))
        return x[:, :128], x[:, 128:]

    cosines, sines = [wide(c) for c in cosines], [wide(s) for s in sines]
    lax.fori_loop(0, count, chunk, 0)


def rows_at(k, rows):
    return pl.ds(pl.multiple_of(k * rows, rows), rows)


CHUNK = 256


def first_band(p_ref, out_ref, b_ref, sums_ref):
    def fold(k, carry):
        at = rows_at(k, CHUNK)
        b_ref[at, :128], b_ref[at, 128:] = mirrored(p_ref[at, 256:384], p_ref[at, 384:])
        return carry

    lax.fori_loop(0, p_ref.shape[0] // CHUNK, fold, 0)

    def load(k):
        at = rows_at(k, 8)
        return halves(p_ref, at), halves(b_ref, at)

    band_of(load, p_ref.shape[0] // 8, out_ref, sums_ref)


def second_band(t_ref, b_ref, out_ref, sums_ref):
    def load(k):
        at = rows_at(k, 8)
        return halves(t_ref, at), halves(b_ref, at)

    band_of(load, t_ref.shape[0] // 8, out_ref, sums_ref)


def first_turn(parts_ref, t_ref, b_ref, t_out, b_out, x_ref):
    cosines, sines = angles_of(parts_ref, x_ref)

    def load(k):
        at = rows_at(k, CHUNK)
        return halves(t_ref, at), halves(b_ref, at)

    def store(k, t, b):
        at = rows_at(k, CHUNK)
        t_out[at, :128], t_out[at, 128:] = retreated_top(t, b)
        b_out[at, :128], b_out[at, 128:] = retreated_bottom(t, b)

    turned_chunks(load, store, t_ref.shape[0] // CHUNK, CHUNK, cosines, sines)


def second_turn(parts_ref, t_ref, b_ref, out_ref, x_ref):
    cosines, sines = angles_of(parts_ref, x_ref)

    def load(k):
        at = rows_at(k, CHUNK)
        return halves(t_ref, at), halves(b_ref, at)

    def store(k, t, b):
        at = rows_at(k, CHUNK)
        out_ref[at, :128], out_ref[at, 128:256] = retreated_top(t, b)
        out_ref[at, 256:384], out_ref[at, 384:] = unfolded_bottom(t, b)

    turned_chunks(load, store, t_ref.shape[0] // CHUNK, CHUNK, cosines, sines)


def call(body, outs, args, scratch=()):
    vmem = pl.BlockSpec(memory_space=pltpu.VMEM)
    shapes = [jax.ShapeDtypeStruct(s, f32) for s in outs]
    return pl.pallas_call(
        body,
        out_shape=shapes,
        in_specs=[vmem] * len(args),
        out_specs=[vmem] * len(outs),
        scratch_shapes=[pltpu.VMEM(s, f32) for s in scratch],
        compiler_params=pltpu.CompilerParams(vmem_limit_bytes=32 * 1024 * 1024),
        interpret=INTERPRET,
    )(*args)


NEAR, FAR = ("near",), ("far", "side")


def exchanged(parts, near, far):
    arrived = lax.all_to_all(parts, NEAR, 0, 0, tiled=True)
    total = arrived[0]
    for k in range(1, near):
        total = total + arrived[k]
    again = jnp.broadcast_to(total[None], (far, *total.shape))
    return lax.all_to_all(again, FAR, 0, 0, tiled=True)


SUMS = [(8 * LINES, 128)]
STATE = [(4, DIAGS, HALF)]


def per_device(snapshots, near, far, groups):
    rows = snapshots.shape[0]
    square, band = (rows, HALF), (near, LINES, 128)
    parts, b = call(first_band, [band, square], [snapshots], SUMS)
    t, b = call(first_turn, [square, square], [exchanged(parts, near, far), snapshots, b], STATE)
    b = lax.ppermute(b, "grp", [(i, (i + 1) % groups) for i in range(groups)])
    (parts,) = call(second_band, [band], [t, b], SUMS)
    (out,) = call(second_turn, [(rows, 2 * HALF)], [exchanged(parts, near, far), t, b], STATE)
    return out


def solution(mesh):
    groups, rows = mesh.shape["grp"], mesh.shape["row"]
    near, side = 4, 2
    far = rows // (near * side)
    fine = Mesh(mesh.devices.reshape(groups, far, near, side), ("grp", "far", "near", "side"))
    placed = P(("far", "near", "side"), "grp")
    body = functools.partial(per_device, near=near, far=far * side, groups=groups)
    return jax.shard_map(body, mesh=fine, in_specs=(placed,), out_specs=placed, check_vma=False)
```

```python
import functools

import jax
import jax.numpy as jnp
from jax import lax
from jax.experimental import pallas as pl
from jax.experimental.pallas import tpu as pltpu
from jax.sharding import Mesh
from jax.sharding import PartitionSpec as P

ROUNDS = 6
HALF = 256
REACH = 10
DIAGS = 24
MID = 12
WIDE = 23
LINES = 48
WINDOW = 16

f32 = jnp.float32
INTERPRET = False


def lanes(shape):
    return lax.broadcasted_iota(jnp.int32, shape, 1)


def turn_lanes(x, by):
    by %= x.shape[1]
    return pltpu.roll(x, by, axis=1) if by else x


def turn_lines(x, by):
    return pltpu.roll(x, by % x.shape[0], axis=0)


def picked(x, index):
    return jnp.take_along_axis(x, index, axis=1, mode="promise_in_bounds")


def mirrored(low, high):
    index = 127 - lanes(low.shape)
    return picked(high, index), picked(low, index)


def ends(t, b):
    at = lanes(t[0].shape)
    e = jnp.where(
        at < 16,
        t[0],
        jnp.where(at < 32, turn_lanes(t[1], 26), jnp.where(at < 48, turn_lanes(b[0], 32), turn_lanes(b[1], 58))),
    )
    swapped = jnp.where(at < 96, turn_lanes(e, 32), turn_lanes(e, 96))
    return jnp.where(at < 64, e, turn_lanes(e, 64)), jnp.where(at < 64, e, swapped)


def place_of_odd(shape):
    k = lax.broadcasted_iota(jnp.int32, shape, 0)
    return k, REACH // 2 - k, (k * (REACH + 1 - k)) // 2


def packed_odd(sums):
    k, count, start = place_of_odd(sums.shape)
    at = lanes(sums.shape)
    inside = at % WINDOW - start
    first = jnp.where((at // WINDOW) % 2 == 0, 0, REACH // 2 - 1 - k)
    index = jnp.clip(at - at % WINDOW + first + inside, 0, 127)
    used = (k < REACH // 2) & (inside >= 0) & (inside < count)
    return jnp.sum(jnp.where(used, picked(sums, index), 0.0), axis=0, keepdims=True)


def unpacked_odd(line, window, mirror):
    line = jnp.broadcast_to(line, (8, 128))
    k, count, start = place_of_odd(line.shape)
    at = lanes(line.shape) - (2 * k + 1 if mirror else 0)
    out = []
    for end in range(2):
        inside = at - (128 - REACH + REACH // 2 - 1 - k if end else 0)
        used = (k < REACH // 2) & (inside >= 0) & (inside < count)
        index = jnp.clip((window + end) * WINDOW + start + inside, 0, 127)
        out.append(jnp.where(used, picked(line, index), 0.0))
    return jnp.concatenate(out, axis=1)


def ahead(x, d):
    low, high = (turn_lanes(half, -d) for half in x)
    return jnp.where(lanes(low.shape) < 128 - d, low, high), high


def halves(ref, at):
    return ref[at, :128], ref[at, 128:256]


def band_of(load, count, out_ref, sums_ref):
    def over_rows(step, n, width):
        zeros = tuple(jnp.zeros((8, 128), f32) for _ in range(n * width))
        return lax.fori_loop(0, count, lambda k, sums: step(*load(k), sums), zeros, unroll=16)

    def with_top(t, b, sums):
        new = []
        for d in range(0, REACH + 1, 2):
            shifted = ahead(t, d) if d else t
            for left in (t, b) if d else (t,):
                new += [left[h] * shifted[h] for h in range(2)]
        return tuple(x + y for x, y in zip(sums, new))

    def with_bottom(t, b, sums):
        new = []
        for d in range(0, REACH + 1, 2):
            shifted = ahead(b, d) if d else b
            for left in (b, t):
                new += [left[h] * shifted[h] for h in range(2)]
        return tuple(x + y for x, y in zip(sums, new))

    def at_ends(t, b, sums):
        left, right = ends(t, b)
        new = [left * turn_lanes(right, -d) for d in range(1, REACH, 2)]
        return tuple(x + y for x, y in zip(sums, new))

    def keep(line, value):
        sums_ref[pl.ds(8 * line, 8), :] = value

    sums = over_rows(with_top, 11, 2)
    for h in range(2):
        keep(24 * h, sums[h])
        for j in range(1, 6):
            keep(24 * h + j, sums[4 * j - 2 + h])
            keep(24 * h + 17 + j, sums[4 * j + h])
    sums = over_rows(with_bottom, 12, 2)
    for h in range(2):
        for j in range(6):
            keep(24 * h + 6 + j, sums[4 * j + h])
            keep(24 * h + 12 + j, sums[4 * j + 2 + h])
    sums = over_rows(at_ends, 5, 1)
    for j in range(5):
        keep(LINES + j, sums[j])
    for line in (WIDE, LINES - 1, LINES + 5, LINES + 6, LINES + 7):
        keep(line, jnp.zeros((8, 128), f32))
    parts = [sums_ref[pl.ds(k, LINES + 8, stride=8), :] for k in range(8)]
    while len(parts) > 1:
        parts = [x + y for x, y in zip(parts[::2], parts[1::2])]
    odd = packed_odd(parts[0][LINES:])
    for k in range(out_ref.shape[0]):
        out_ref[k] = parts[0][:LINES]
        out_ref[k, WIDE : WIDE + 1, :] = odd


def along_columns(x):
    shifted = jnp.broadcast_to(turn_lanes(x, -MID), (DIAGS, HALF))
    return pltpu.roll(shifted, 0, axis=1, stride=1, stride_axis=0)


def angles_of(parts_ref, x_ref):
    band = parts_ref[0]
    for k in range(1, parts_ref.shape[0]):
        band = band + parts_ref[k]
    low, high = band[:24], band[24:]
    blank = jnp.zeros((1, HALF), f32)
    for block in range(4):
        for line in (0, DIAGS - 2, DIAGS - 1):
            x_ref[block, line : line + 1, :] = blank
    TT, TB, BT, BB = 0, 1, 2, 3

    def put(block, other, d, value):
        x_ref[block, MID - d : MID - d + 1, :] = value
        x_ref[other, MID + d : MID + d + 1, :] = turn_lanes(value, d)

    def line(k):
        return jnp.concatenate([low[k : k + 1], high[k : k + 1]], axis=1)

    for j in range(6):
        put(TT, TT, 2 * j, line(j))
        put(BB, BB, 2 * j, line(6 + j))
        put(TB, BT, 2 * j, line(12 + j))
        if j:
            put(BT, TB, 2 * j, line(17 + j))
    for window, (block, other) in enumerate(((TT, TT), (BB, BB), (TB, BT), (BT, TB))):
        there = unpacked_odd(low[WIDE : WIDE + 1], 2 * window, False)
        mirror = unpacked_odd(low[WIDE : WIDE + 1], 2 * window, True)
        for j in range(5):
            d = 2 * j + 1
            x_ref[block, MID - d : MID - d + 1, :] = there[j : j + 1]
            x_ref[other, MID + d : MID + d + 1, :] = mirror[j : j + 1]

    tt, tb, bt, bb = (x_ref[k] for k in range(4))
    shape = (DIAGS, HALF)
    i = lanes(shape)
    j = i + MID - lax.broadcasted_iota(jnp.int32, shape, 0)
    i_one, i_more, i_last = i == 1, i >= 2, i == HALF - 1
    j_one, j_more, j_last = j == 1, j >= 2, j == HALF - 1

    def less(x):
        return turn_lines(x, -1)

    def more(x):
        return turn_lines(x, 1)

    cosines, sines = [], []
    for turn in range(ROUNDS):
        first, second, coupling = (x[MID : MID + 1] for x in (tt, bb, tb))
        difference = second - first
        direction = jnp.where(difference >= 0, 1.0, -1.0)
        denominator = (
            jnp.abs(difference)
            + jnp.sqrt(difference * difference + 4.0 * coupling * coupling)
            + 1e-06 * (first + second)
        )
        tangent = direction * 2.0 * coupling / denominator
        c = 1.0 / jnp.sqrt(1.0 + tangent * tangent)
        s = tangent * c
        cosines.append(c)
        sines.append(s)
        if turn == ROUNDS - 1:
            break
        c_row, s_row = jnp.broadcast_to(c, shape), jnp.broadcast_to(s, shape)
        c_col, s_col = along_columns(c), along_columns(s)
        tt, tb = c_col * tt - s_col * tb, s_col * tt + c_col * tb
        bt, bb = c_col * bt - s_col * bb, s_col * bt + c_col * bb
        tt, bt = c_row * tt - s_row * bt, s_row * tt + c_row * bt
        tb, bb = c_row * tb - s_row * bb, s_row * tb + c_row * bb
        tt, tb = (
            jnp.where(j_more, less(tt), jnp.where(j_one, less(tb), tt)),
            jnp.where(j_last, tt, more(tb)),
        )
        bt, bb = (
            jnp.where(j_more, less(bt), jnp.where(j_one, less(bb), bt)),
            jnp.where(j_last, bt, more(bb)),
        )
        tt, bt = (
            jnp.where(i_more, turn_lanes(more(tt), 1), jnp.where(i_one, turn_lanes(more(bt), 1), tt)),
            jnp.where(i_last, tt, turn_lanes(less(bt), -1)),
        )
        tb, bb = (
            jnp.where(i_more, turn_lanes(more(tb), 1), jnp.where(i_one, turn_lanes(more(bb), 1), tb)),
            jnp.where(i_last, tb, turn_lanes(less(bb), -1)),
        )
    return cosines, sines


def advanced(t, b):
    at = lanes(t[0].shape)
    t0, t1, b0, b1 = turn_lanes(t[0], 1), turn_lanes(t[1], 1), turn_lanes(b[0], -1), turn_lanes(b[1], -1)
    return (
        (
            jnp.where(at >= 2, t0, jnp.where(at == 1, turn_lanes(b[0], 1), t[0])),
            jnp.where(at >= 1, t1, t0),
        ),
        (jnp.where(at == 127, b1, b0), jnp.where(at == 127, t[1], b1)),
    )


MOVES = ROUNDS - 1


def retreated_top(t, b):
    at = lanes(t[0].shape)
    back = [turn_lanes(x, -MOVES) for x in t]
    from_bottom = picked(b[1], (250 - at) % 128)
    return (
        jnp.where(at == 0, t[0], jnp.where(at < 128 - MOVES, back[0], back[1])),
        jnp.where(at < 128 - MOVES, back[1], from_bottom),
    )


def retreated_bottom(t, b):
    at = lanes(t[0].shape)
    on = [turn_lanes(x, MOVES) for x in b]
    from_top = picked(t[0], (MOVES - at) % 128)
    return (
        jnp.where(at < MOVES, from_top, on[0]),
        jnp.where(at < MOVES, on[0], on[1]),
    )


def unfolded_bottom(t, b):
    at = lanes(t[0].shape)
    index = (122 - at) % 128
    low, high = picked(b[0], index), picked(b[1], index)
    return (
        jnp.where(at <= 122, high, low),
        jnp.where(at <= 122, low, turn_lanes(t[0], 122)),
    )


def turned_chunks(load, store, count, rows, cosines, sines):
    def chunk(k, carry):
        t, b = load(k)
        for turn in range(ROUNDS):
            c, s = cosines[turn], sines[turn]
            t, b = (
                tuple(c[h] * t[h] - s[h] * b[h] for h in range(2)),
                tuple(s[h] * t[h] + c[h] * b[h] for h in range(2)),
            )
            if turn < MOVES:
                t, b = advanced(t, b)
        store(k, t, b)
        return carry

    def wide(x):
        x = jnp.broadcast_to(x, (rows, HALF))
        return x[:, :128], x[:, 128:]

    cosines, sines = [wide(c) for c in cosines], [wide(s) for s in sines]
    lax.fori_loop(0, count, chunk, 0)


def rows_at(k, rows):
    return pl.ds(pl.multiple_of(k * rows, rows), rows)


CHUNK = 256


def first_band(p_ref, out_ref, b_ref, sums_ref):
    def fold(k, carry):
        at = rows_at(k, CHUNK)
        b_ref[at, :128], b_ref[at, 128:] = mirrored(p_ref[at, 256:384], p_ref[at, 384:])
        return carry

    lax.fori_loop(0, p_ref.shape[0] // CHUNK, fold, 0)

    def load(k):
        at = rows_at(k, 8)
        return halves(p_ref, at), halves(b_ref, at)

    band_of(load, p_ref.shape[0] // 8, out_ref, sums_ref)


def second_band(t_ref, b_ref, out_ref, sums_ref):
    def load(k):
        at = rows_at(k, 8)
        return halves(t_ref, at), halves(b_ref, at)

    band_of(load, t_ref.shape[0] // 8, out_ref, sums_ref)


def first_turn(parts_ref, t_ref, b_ref, t_out, b_out, x_ref):
    cosines, sines = angles_of(parts_ref, x_ref)

    def load(k):
        at = rows_at(k, CHUNK)
        return halves(t_ref, at), halves(b_ref, at)

    def store(k, t, b):
        at = rows_at(k, CHUNK)
        t_out[at, :128], t_out[at, 128:] = retreated_top(t, b)
        b_out[at, :128], b_out[at, 128:] = retreated_bottom(t, b)

    turned_chunks(load, store, t_ref.shape[0] // CHUNK, CHUNK, cosines, sines)


def second_turn(parts_ref, t_ref, b_ref, out_ref, x_ref):
    cosines, sines = angles_of(parts_ref, x_ref)

    def load(k):
        at = rows_at(k, CHUNK)
        return halves(t_ref, at), halves(b_ref, at)

    def store(k, t, b):
        at = rows_at(k, CHUNK)
        out_ref[at, :128], out_ref[at, 128:256] = retreated_top(t, b)
        out_ref[at, 256:384], out_ref[at, 384:] = unfolded_bottom(t, b)

    turned_chunks(load, store, t_ref.shape[0] // CHUNK, CHUNK, cosines, sines)


def call(body, outs, args, scratch=()):
    vmem = pl.BlockSpec(memory_space=pltpu.VMEM)
    shapes = [jax.ShapeDtypeStruct(s, f32) for s in outs]
    return pl.pallas_call(
        body,
        out_shape=shapes,
        in_specs=[vmem] * len(args),
        out_specs=[vmem] * len(outs),
        scratch_shapes=[pltpu.VMEM(s, f32) for s in scratch],
        compiler_params=pltpu.CompilerParams(vmem_limit_bytes=32 * 1024 * 1024),
        interpret=INTERPRET,
    )(*args)


NEAR, FAR = "near", "far"


def exchanged(parts, near, far):
    arrived = lax.all_to_all(parts, NEAR, 0, 0, tiled=True)
    total = arrived[0]
    for k in range(1, near):
        total = total + arrived[k]
    again = jnp.broadcast_to(total[None], (far, *total.shape))
    return lax.all_to_all(again, FAR, 0, 0, tiled=True)


SUMS = [(8 * LINES + 64, 128)]
STATE = [(4, DIAGS, HALF)]


def per_device(snapshots, near, far, groups):
    rows = snapshots.shape[0]
    square, band = (rows, HALF), (near, LINES, 128)
    parts, b = call(first_band, [band, square], [snapshots], SUMS)
    t, b = call(first_turn, [square, square], [exchanged(parts, near, far), snapshots, b], STATE)
    b = lax.ppermute(b, "grp", [(i, (i + 1) % groups) for i in range(groups)])
    (parts,) = call(second_band, [band], [t, b], SUMS)
    (out,) = call(second_turn, [(rows, 2 * HALF)], [exchanged(parts, near, far), t, b], STATE)
    return out


def solution(mesh):
    groups, rows = mesh.shape["grp"], mesh.shape["row"]
    near, far = 4, rows // 4
    fine = Mesh(mesh.devices.reshape(groups, far, near), ("grp", "far", "near"))
    placed = P(("far", "near"), "grp")
    body = functools.partial(per_device, near=near, far=far, groups=groups)
    return jax.shard_map(body, mesh=fine, in_specs=(placed,), out_specs=placed, check_vma=False)
```

```python
import functools

import jax
import jax.numpy as jnp
from jax import lax
from jax.experimental import pallas as pl
from jax.experimental.pallas import tpu as pltpu
from jax.sharding import Mesh
from jax.sharding import PartitionSpec as P

ROUNDS = 6
HALF = 256
REACH = 10
DIAGS = 24
MID = 12
WIDE = 23
LINES = 48
WINDOW = 16

f32 = jnp.float32
INTERPRET = False


def lanes(shape):
    return lax.broadcasted_iota(jnp.int32, shape, 1)


def turn_lanes(x, by):
    by %= x.shape[1]
    return pltpu.roll(x, by, axis=1) if by else x


def turn_lines(x, by):
    return pltpu.roll(x, by % x.shape[0], axis=0)


def picked(x, index):
    return jnp.take_along_axis(x, index, axis=1, mode="promise_in_bounds")


def mirrored(low, high):
    index = 127 - lanes(low.shape)
    return picked(high, index), picked(low, index)


def ends(t, b):
    at = lanes(t[0].shape)
    e = jnp.where(
        at < 16,
        t[0],
        jnp.where(at < 32, turn_lanes(t[1], 26), jnp.where(at < 48, turn_lanes(b[0], 32), turn_lanes(b[1], 58))),
    )
    swapped = jnp.where(at < 96, turn_lanes(e, 32), turn_lanes(e, 96))
    return jnp.where(at < 64, e, turn_lanes(e, 64)), jnp.where(at < 64, e, swapped)


def place_of_odd(shape):
    k = lax.broadcasted_iota(jnp.int32, shape, 0)
    return k, REACH // 2 - k, (k * (REACH + 1 - k)) // 2


def packed_odd(sums):
    k, count, start = place_of_odd(sums.shape)
    at = lanes(sums.shape)
    inside = at % WINDOW - start
    first = jnp.where((at // WINDOW) % 2 == 0, 0, REACH // 2 - 1 - k)
    index = jnp.clip(at - at % WINDOW + first + inside, 0, 127)
    used = (k < REACH // 2) & (inside >= 0) & (inside < count)
    return jnp.sum(jnp.where(used, picked(sums, index), 0.0), axis=0, keepdims=True)


def unpacked_odd(line, window, mirror):
    line = jnp.broadcast_to(line, (8, 128))
    k, count, start = place_of_odd(line.shape)
    at = lanes(line.shape) - (2 * k + 1 if mirror else 0)
    out = []
    for end in range(2):
        inside = at - (128 - REACH + REACH // 2 - 1 - k if end else 0)
        used = (k < REACH // 2) & (inside >= 0) & (inside < count)
        index = jnp.clip((window + end) * WINDOW + start + inside, 0, 127)
        out.append(jnp.where(used, picked(line, index), 0.0))
    return jnp.concatenate(out, axis=1)


def ahead(x, d):
    low, high = (turn_lanes(half, -d) for half in x)
    return jnp.where(lanes(low.shape) < 128 - d, low, high), high


def halves(ref, at):
    return ref[at, :128], ref[at, 128:256]


def band_of(load, count, out_ref, sums_ref):
    def over_rows(step, n, width):
        zeros = tuple(jnp.zeros((8, 128), f32) for _ in range(n * width))
        return lax.fori_loop(0, count, lambda k, sums: step(*load(k), sums), zeros, unroll=16)

    def with_top(t, b, sums):
        new = []
        for d in range(0, REACH + 1, 2):
            shifted = ahead(t, d) if d else t
            for left in (t, b) if d else (t,):
                new += [left[h] * shifted[h] for h in range(2)]
        return tuple(x + y for x, y in zip(sums, new))

    def with_bottom(t, b, sums):
        new = []
        for d in range(0, REACH + 1, 2):
            shifted = ahead(b, d) if d else b
            for left in (b, t):
                new += [left[h] * shifted[h] for h in range(2)]
        return tuple(x + y for x, y in zip(sums, new))

    def at_ends(t, b, sums):
        left, right = ends(t, b)
        new = [left * turn_lanes(right, -d) for d in range(1, REACH, 2)]
        return tuple(x + y for x, y in zip(sums, new))

    def keep(line, value):
        sums_ref[pl.ds(8 * line, 8), :] = value

    sums = over_rows(with_top, 11, 2)
    for h in range(2):
        keep(24 * h, sums[h])
        for j in range(1, 6):
            keep(24 * h + j, sums[4 * j - 2 + h])
            keep(24 * h + 17 + j, sums[4 * j + h])
    sums = over_rows(with_bottom, 12, 2)
    for h in range(2):
        for j in range(6):
            keep(24 * h + 6 + j, sums[4 * j + h])
            keep(24 * h + 12 + j, sums[4 * j + 2 + h])
    sums = over_rows(at_ends, 5, 1)
    for j in range(5):
        keep(LINES + j, sums[j])
    for line in (WIDE, LINES - 1, LINES + 5, LINES + 6, LINES + 7):
        keep(line, jnp.zeros((8, 128), f32))
    parts = [sums_ref[pl.ds(k, LINES + 8, stride=8), :] for k in range(8)]
    while len(parts) > 1:
        parts = [x + y for x, y in zip(parts[::2], parts[1::2])]
    odd = packed_odd(parts[0][LINES:])
    for k in range(out_ref.shape[0]):
        out_ref[k] = parts[0][:LINES]
        out_ref[k, WIDE : WIDE + 1, :] = odd


def along_columns(x):
    shifted = jnp.broadcast_to(turn_lanes(x, -MID), (DIAGS, HALF))
    return pltpu.roll(shifted, 0, axis=1, stride=1, stride_axis=0)


def angles_of(parts_ref, x_ref):
    band = parts_ref[0]
    for k in range(1, parts_ref.shape[0]):
        band = band + parts_ref[k]
    low, high = band[:24], band[24:]
    blank = jnp.zeros((1, HALF), f32)
    for block in range(4):
        for line in (0, DIAGS - 2, DIAGS - 1):
            x_ref[block, line : line + 1, :] = blank
    TT, TB, BT, BB = 0, 1, 2, 3

    def put(block, other, d, value):
        x_ref[block, MID - d : MID - d + 1, :] = value
        x_ref[other, MID + d : MID + d + 1, :] = turn_lanes(value, d)

    def line(k):
        return jnp.concatenate([low[k : k + 1], high[k : k + 1]], axis=1)

    for j in range(6):
        put(TT, TT, 2 * j, line(j))
        put(BB, BB, 2 * j, line(6 + j))
        put(TB, BT, 2 * j, line(12 + j))
        if j:
            put(BT, TB, 2 * j, line(17 + j))
    for window, (block, other) in enumerate(((TT, TT), (BB, BB), (TB, BT), (BT, TB))):
        there = unpacked_odd(low[WIDE : WIDE + 1], 2 * window, False)
        mirror = unpacked_odd(low[WIDE : WIDE + 1], 2 * window, True)
        for j in range(5):
            d = 2 * j + 1
            x_ref[block, MID - d : MID - d + 1, :] = there[j : j + 1]
            x_ref[other, MID + d : MID + d + 1, :] = mirror[j : j + 1]

    tt, tb, bt, bb = (x_ref[k] for k in range(4))
    shape = (DIAGS, HALF)
    i = lanes(shape)
    j = i + MID - lax.broadcasted_iota(jnp.int32, shape, 0)
    i_none, i_one, i_last = i == 0, i == 1, i == HALF - 1
    j_none, j_one, j_last = j == 0, j == 1, j == HALF - 1
    one = lanes((1, HALF))
    one_none, one_one, one_last = one == 0, one == 1, one == HALF - 1

    def less(x, by=1):
        return turn_lines(x, -by)

    def more(x, by=1):
        return turn_lines(x, by)

    def up(x):
        return turn_lanes(x, 1)

    def down(x):
        return turn_lanes(x, -1)

    def both_sides(blocks, c_row, s_row, c_col, s_col):
        tt, tb, bt, bb = blocks
        tt, tb = c_col * tt - s_col * tb, s_col * tt + c_col * tb
        bt, bb = c_col * bt - s_col * bb, s_col * bt + c_col * bb
        tt, bt = c_row * tt - s_row * bt, s_row * tt + c_row * bt
        tb, bb = c_row * tb - s_row * bb, s_row * tb + c_row * bb
        return tt, tb, bt, bb

    cosines, sines = [], []
    blocks = tt, tb, bt, bb
    first, second, coupling = (x[MID : MID + 1] for x in (tt, bb, tb))
    for turn in range(ROUNDS):
        difference = second - first
        direction = jnp.where(difference >= 0, 1.0, -1.0)
        denominator = (
            jnp.abs(difference)
            + jnp.sqrt(difference * difference + 4.0 * coupling * coupling)
            + 1e-06 * (first + second)
        )
        tangent = direction * 2.0 * coupling / denominator
        c = lax.rsqrt(1.0 + tangent * tangent)
        s = tangent * c
        cosines.append(c)
        sines.append(s)
        if turn == ROUNDS - 1:
            break
        here = both_sides([x[MID : MID + 1] for x in blocks], c, s, c, s)
        next_one = both_sides([x[MID - 1 : MID] for x in blocks], c, s, down(c), down(s))
        next_two = both_sides([x[MID - 2 : MID - 1] for x in blocks], c, s, turn_lanes(c, -2), turn_lanes(s, -2))
        first = jnp.where(one_none, here[0], jnp.where(one_one, up(here[3]), up(here[0])))
        second = jnp.where(one_last, here[0], down(here[3]))
        coupling = jnp.where(
            one_none,
            next_one[1],
            jnp.where(one_one, up(next_two[3]), jnp.where(one_last, up(next_one[0]), up(next_two[1]))),
        )
        if turn == ROUNDS - 2:
            continue
        tt, tb, bt, bb = both_sides(
            blocks,
            jnp.broadcast_to(c, shape),
            jnp.broadcast_to(s, shape),
            along_columns(c),
            along_columns(s),
        )
        column, corner = jnp.where(j_none, tb, tt), jnp.where(j_none, bb, bt)
        blocks = (
            jnp.where(
                i_none,
                jnp.where(j_none, tt, less(column)),
                jnp.where(j_none, up(more(jnp.where(i_none, bt, tt))), up(jnp.where(i_none, corner, column))),
            ),
            jnp.where(
                i_none,
                more(tb),
                jnp.where(j_last, up(more(tt)), up(more(jnp.where(i_none, bb, tb), 2))),
            ),
            jnp.where(
                i_last,
                less(tt),
                jnp.where(
                    j_none, down(less(bt)), jnp.where(j_one, down(less(bb, 2)), down(less(bt, 2)))
                ),
            ),
            jnp.where(
                i_last,
                jnp.where(j_last, tt, more(tb)),
                jnp.where(j_last, down(less(bt)), down(bb)),
            ),
        )
    return cosines, sines


def advanced(t, b):
    at = lanes(t[0].shape)
    t0, t1, b0, b1 = turn_lanes(t[0], 1), turn_lanes(t[1], 1), turn_lanes(b[0], -1), turn_lanes(b[1], -1)
    return (
        (
            jnp.where(at >= 2, t0, jnp.where(at == 1, turn_lanes(b[0], 1), t[0])),
            jnp.where(at >= 1, t1, t0),
        ),
        (jnp.where(at == 127, b1, b0), jnp.where(at == 127, t[1], b1)),
    )


MOVES = ROUNDS - 1


def retreated_top(t, b):
    at = lanes(t[0].shape)
    back = [turn_lanes(x, -MOVES) for x in t]
    from_bottom = picked(b[1], (250 - at) % 128)
    return (
        jnp.where(at == 0, t[0], jnp.where(at < 128 - MOVES, back[0], back[1])),
        jnp.where(at < 128 - MOVES, back[1], from_bottom),
    )


def retreated_bottom(t, b):
    at = lanes(t[0].shape)
    on = [turn_lanes(x, MOVES) for x in b]
    from_top = picked(t[0], (MOVES - at) % 128)
    return (
        jnp.where(at < MOVES, from_top, on[0]),
        jnp.where(at < MOVES, on[0], on[1]),
    )


def unfolded_bottom(t, b):
    at = lanes(t[0].shape)
    index = (122 - at) % 128
    low, high = picked(b[0], index), picked(b[1], index)
    return (
        jnp.where(at <= 122, high, low),
        jnp.where(at <= 122, low, turn_lanes(t[0], 122)),
    )


def turned_chunks(load, store, count, rows, cosines, sines):
    def chunk(k, carry):
        t, b = load(k)
        for turn in range(ROUNDS):
            c, s = cosines[turn], sines[turn]
            t, b = (
                tuple(c[h] * t[h] - s[h] * b[h] for h in range(2)),
                tuple(s[h] * t[h] + c[h] * b[h] for h in range(2)),
            )
            if turn < MOVES:
                t, b = advanced(t, b)
        store(k, t, b)
        return carry

    def wide(x):
        x = jnp.broadcast_to(x, (rows, HALF))
        return x[:, :128], x[:, 128:]

    cosines, sines = [wide(c) for c in cosines], [wide(s) for s in sines]
    lax.fori_loop(0, count, chunk, 0)


def rows_at(k, rows):
    return pl.ds(pl.multiple_of(k * rows, rows), rows)


CHUNK = 256


def first_band(p_ref, out_ref, b_ref, sums_ref):
    def fold(k, carry):
        at = rows_at(k, CHUNK)
        b_ref[at, :128], b_ref[at, 128:] = mirrored(p_ref[at, 256:384], p_ref[at, 384:])
        return carry

    lax.fori_loop(0, p_ref.shape[0] // CHUNK, fold, 0)

    def load(k):
        at = rows_at(k, 8)
        return halves(p_ref, at), halves(b_ref, at)

    band_of(load, p_ref.shape[0] // 8, out_ref, sums_ref)


def second_band(t_ref, b_ref, out_ref, sums_ref):
    def load(k):
        at = rows_at(k, 8)
        return halves(t_ref, at), halves(b_ref, at)

    band_of(load, t_ref.shape[0] // 8, out_ref, sums_ref)


def first_turn(parts_ref, t_ref, b_ref, t_out, b_out, x_ref):
    cosines, sines = angles_of(parts_ref, x_ref)

    def load(k):
        at = rows_at(k, CHUNK)
        return halves(t_ref, at), halves(b_ref, at)

    def store(k, t, b):
        at = rows_at(k, CHUNK)
        t_out[at, :128], t_out[at, 128:] = retreated_top(t, b)
        b_out[at, :128], b_out[at, 128:] = retreated_bottom(t, b)

    turned_chunks(load, store, t_ref.shape[0] // CHUNK, CHUNK, cosines, sines)


def second_turn(parts_ref, t_ref, b_ref, out_ref, x_ref):
    cosines, sines = angles_of(parts_ref, x_ref)

    def load(k):
        at = rows_at(k, CHUNK)
        return halves(t_ref, at), halves(b_ref, at)

    def store(k, t, b):
        at = rows_at(k, CHUNK)
        out_ref[at, :128], out_ref[at, 128:256] = retreated_top(t, b)
        out_ref[at, 256:384], out_ref[at, 384:] = unfolded_bottom(t, b)

    turned_chunks(load, store, t_ref.shape[0] // CHUNK, CHUNK, cosines, sines)


def call(body, outs, args, scratch=()):
    vmem = pl.BlockSpec(memory_space=pltpu.VMEM)
    shapes = [jax.ShapeDtypeStruct(s, f32) for s in outs]
    return pl.pallas_call(
        body,
        out_shape=shapes,
        in_specs=[vmem] * len(args),
        out_specs=[vmem] * len(outs),
        scratch_shapes=[pltpu.VMEM(s, f32) for s in scratch],
        compiler_params=pltpu.CompilerParams(vmem_limit_bytes=32 * 1024 * 1024),
        interpret=INTERPRET,
    )(*args)


NEAR, FAR = "near", "far"


def exchanged(parts, near, far):
    arrived = lax.all_to_all(parts, NEAR, 0, 0, tiled=True)
    total = arrived[0]
    for k in range(1, near):
        total = total + arrived[k]
    again = jnp.broadcast_to(total[None], (far, *total.shape))
    return lax.all_to_all(again, FAR, 0, 0, tiled=True)


SUMS = [(8 * LINES + 64, 128)]
STATE = [(4, DIAGS, HALF)]


def per_device(snapshots, near, far, groups):
    rows = snapshots.shape[0]
    square, band = (rows, HALF), (near, LINES, 128)
    parts, b = call(first_band, [band, square], [snapshots], SUMS)
    t, b = call(first_turn, [square, square], [exchanged(parts, near, far), snapshots, b], STATE)
    b = lax.ppermute(b, "grp", [(i, (i + 1) % groups) for i in range(groups)])
    (parts,) = call(second_band, [band], [t, b], SUMS)
    (out,) = call(second_turn, [(rows, 2 * HALF)], [exchanged(parts, near, far), t, b], STATE)
    return out


def solution(mesh):
    groups, rows = mesh.shape["grp"], mesh.shape["row"]
    near, far = 4, rows // 4
    fine = Mesh(mesh.devices.reshape(groups, far, near), ("grp", "far", "near"))
    placed = P(("far", "near"), "grp")
    body = functools.partial(per_device, near=near, far=far, groups=groups)
    return jax.shard_map(body, mesh=fine, in_specs=(placed,), out_specs=placed, check_vma=False)
```

```python
import functools

import jax
import jax.numpy as jnp
from jax import lax
from jax.experimental import pallas as pl
from jax.experimental.pallas import tpu as pltpu
from jax.sharding import Mesh
from jax.sharding import PartitionSpec as P

ROUNDS = 6
HALF = 256
REACH = 10
DIAGS = 24
MID = 12
WIDE = 23
LINES = 48
WINDOW = 16

f32 = jnp.float32
INTERPRET = False


def lanes(shape):
    return lax.broadcasted_iota(jnp.int32, shape, 1)


def turn_lanes(x, by):
    by %= x.shape[1]
    return pltpu.roll(x, by, axis=1) if by else x


def turn_lines(x, by):
    return pltpu.roll(x, by % x.shape[0], axis=0)


def picked(x, index):
    return jnp.take_along_axis(x, index, axis=1, mode="promise_in_bounds")


def mirrored(low, high):
    index = 127 - lanes(low.shape)
    return picked(high, index), picked(low, index)


def ends(t, b):
    at = lanes(t[0].shape)
    e = jnp.where(
        at < 16,
        t[0],
        jnp.where(at < 32, turn_lanes(t[1], 26), jnp.where(at < 48, turn_lanes(b[0], 32), turn_lanes(b[1], 58))),
    )
    swapped = jnp.where(at < 96, turn_lanes(e, 32), turn_lanes(e, 96))
    return jnp.where(at < 64, e, turn_lanes(e, 64)), jnp.where(at < 64, e, swapped)


def place_of_odd(shape):
    k = lax.broadcasted_iota(jnp.int32, shape, 0)
    return k, REACH // 2 - k, (k * (REACH + 1 - k)) // 2


def packed_odd(sums):
    k, count, start = place_of_odd(sums.shape)
    at = lanes(sums.shape)
    inside = at % WINDOW - start
    first = jnp.where((at // WINDOW) % 2 == 0, 0, REACH // 2 - 1 - k)
    index = jnp.clip(at - at % WINDOW + first + inside, 0, 127)
    used = (k < REACH // 2) & (inside >= 0) & (inside < count)
    return jnp.sum(jnp.where(used, picked(sums, index), 0.0), axis=0, keepdims=True)


def unpacked_odd(line, window, mirror):
    line = jnp.broadcast_to(line, (8, 128))
    k, count, start = place_of_odd(line.shape)
    at = lanes(line.shape) - (2 * k + 1 if mirror else 0)
    out = []
    for end in range(2):
        inside = at - (128 - REACH + REACH // 2 - 1 - k if end else 0)
        used = (k < REACH // 2) & (inside >= 0) & (inside < count)
        index = jnp.clip((window + end) * WINDOW + start + inside, 0, 127)
        out.append(jnp.where(used, picked(line, index), 0.0))
    return jnp.concatenate(out, axis=1)


def ahead(x, d):
    low, high = (turn_lanes(half, -d) for half in x)
    return jnp.where(lanes(low.shape) < 128 - d, low, high), high


def halves(ref, at):
    return ref[at, :128], ref[at, 128:256]


def over_rows(load, count, step, n):
    zeros = (jnp.zeros((8, 128), f32),) * n
    return lax.fori_loop(0, count, lambda k, sums: step(*load(k), sums), zeros, unroll=16)


def top_band_of(load, count, top_ref):
    def step(t, sums):
        new = []
        for d in range(0, REACH + 1, 2):
            shifted = ahead(t, d) if d else t
            new += [t[h] * shifted[h] for h in range(2)]
        return tuple(x + y for x, y in zip(sums, new))

    sums = over_rows(lambda k: (load(k),), count, step, 12)
    for h in range(2):
        for j in range(6):
            top_ref[pl.ds(48 * h + 8 * j, 8), :] = sums[2 * j + h]


def band_of(load, count, out_ref, sums_ref, top_ref=None):
    def with_top(t, b, sums):
        new = []
        for d in range(2 if top_ref is not None else 0, REACH + 1, 2):
            shifted = ahead(t, d) if d else t
            if top_ref is None:
                new += [t[h] * shifted[h] for h in range(2)]
            if d:
                new += [b[h] * shifted[h] for h in range(2)]
        return tuple(x + y for x, y in zip(sums, new))

    def with_bottom(t, b, sums):
        new = []
        for d in range(0, REACH + 1, 2):
            shifted = ahead(b, d) if d else b
            for left in (b, t):
                new += [left[h] * shifted[h] for h in range(2)]
        return tuple(x + y for x, y in zip(sums, new))

    def at_ends(t, b, sums):
        left, right = ends(t, b)
        new = [left * turn_lanes(right, -d) for d in range(1, REACH, 2)]
        return tuple(x + y for x, y in zip(sums, new))

    def keep(line, value):
        sums_ref[pl.ds(8 * line, 8), :] = value

    if top_ref is not None:
        sums = over_rows(load, count, with_top, 10)
        for h in range(2):
            sums_ref[pl.ds(8 * 24 * h, 48), :] = top_ref[pl.ds(48 * h, 48), :]
            for j in range(1, 6):
                keep(24 * h + 17 + j, sums[2 * j - 2 + h])
    else:
        sums = over_rows(load, count, with_top, 22)
        for h in range(2):
            keep(24 * h, sums[h])
            for j in range(1, 6):
                keep(24 * h + j, sums[4 * j - 2 + h])
                keep(24 * h + 17 + j, sums[4 * j + h])
    sums = over_rows(load, count, with_bottom, 24)
    for h in range(2):
        for j in range(6):
            keep(24 * h + 6 + j, sums[4 * j + h])
            keep(24 * h + 12 + j, sums[4 * j + 2 + h])
    sums = over_rows(load, count, at_ends, 5)
    for j in range(5):
        keep(LINES + j, sums[j])
    for line in (WIDE, LINES - 1, LINES + 5, LINES + 6, LINES + 7):
        keep(line, jnp.zeros((8, 128), f32))
    parts = [sums_ref[pl.ds(k, LINES + 8, stride=8), :] for k in range(8)]
    while len(parts) > 1:
        parts = [x + y for x, y in zip(parts[::2], parts[1::2])]
    odd = packed_odd(parts[0][LINES:])
    for k in range(out_ref.shape[0]):
        out_ref[k] = parts[0][:LINES]
        out_ref[k, WIDE : WIDE + 1, :] = odd


def along_columns(x):
    shifted = jnp.broadcast_to(turn_lanes(x, -MID), (DIAGS, HALF))
    return pltpu.roll(shifted, 0, axis=1, stride=1, stride_axis=0)


def angles_of(parts_ref, x_ref):
    band = parts_ref[0]
    for k in range(1, parts_ref.shape[0]):
        band = band + parts_ref[k]
    low, high = band[:24], band[24:]
    blank = jnp.zeros((1, HALF), f32)
    for block in range(4):
        for line in (0, DIAGS - 2, DIAGS - 1):
            x_ref[block, line : line + 1, :] = blank
    TT, TB, BT, BB = 0, 1, 2, 3

    def put(block, other, d, value):
        x_ref[block, MID - d : MID - d + 1, :] = value
        x_ref[other, MID + d : MID + d + 1, :] = turn_lanes(value, d)

    def line(k):
        return jnp.concatenate([low[k : k + 1], high[k : k + 1]], axis=1)

    for j in range(6):
        put(TT, TT, 2 * j, line(j))
        put(BB, BB, 2 * j, line(6 + j))
        put(TB, BT, 2 * j, line(12 + j))
        if j:
            put(BT, TB, 2 * j, line(17 + j))
    for window, (block, other) in enumerate(((TT, TT), (BB, BB), (TB, BT), (BT, TB))):
        there = unpacked_odd(low[WIDE : WIDE + 1], 2 * window, False)
        mirror = unpacked_odd(low[WIDE : WIDE + 1], 2 * window, True)
        for j in range(5):
            d = 2 * j + 1
            x_ref[block, MID - d : MID - d + 1, :] = there[j : j + 1]
            x_ref[other, MID + d : MID + d + 1, :] = mirror[j : j + 1]

    tt, tb, bt, bb = (x_ref[k] for k in range(4))
    shape = (DIAGS, HALF)
    i = lanes(shape)
    j = i + MID - lax.broadcasted_iota(jnp.int32, shape, 0)
    i_none, i_one, i_last = i == 0, i == 1, i == HALF - 1
    j_none, j_one, j_last = j == 0, j == 1, j == HALF - 1
    one = lanes((1, HALF))
    one_none, one_one, one_last = one == 0, one == 1, one == HALF - 1

    def less(x, by=1):
        return turn_lines(x, -by)

    def more(x, by=1):
        return turn_lines(x, by)

    def up(x):
        return turn_lanes(x, 1)

    def down(x):
        return turn_lanes(x, -1)

    def both_sides(blocks, c_row, s_row, c_col, s_col):
        tt, tb, bt, bb = blocks
        tt, tb = c_col * tt - s_col * tb, s_col * tt + c_col * tb
        bt, bb = c_col * bt - s_col * bb, s_col * bt + c_col * bb
        tt, bt = c_row * tt - s_row * bt, s_row * tt + c_row * bt
        tb, bb = c_row * tb - s_row * bb, s_row * tb + c_row * bb
        return tt, tb, bt, bb

    cosines, sines = [], []
    blocks = tt, tb, bt, bb
    first, second, coupling = (x[MID : MID + 1] for x in (tt, bb, tb))
    for turn in range(ROUNDS):
        difference = second - first
        direction = jnp.where(difference >= 0, 1.0, -1.0)
        denominator = (
            jnp.abs(difference)
            + jnp.sqrt(difference * difference + 4.0 * coupling * coupling)
            + 1e-06 * (first + second)
        )
        tangent = direction * 2.0 * coupling / denominator
        c = lax.rsqrt(1.0 + tangent * tangent)
        s = tangent * c
        cosines.append(c)
        sines.append(s)
        if turn == ROUNDS - 1:
            break
        here = both_sides([x[MID : MID + 1] for x in blocks], c, s, c, s)
        next_one = both_sides([x[MID - 1 : MID] for x in blocks], c, s, down(c), down(s))
        next_two = both_sides([x[MID - 2 : MID - 1] for x in blocks], c, s, turn_lanes(c, -2), turn_lanes(s, -2))
        first = jnp.where(one_none, here[0], jnp.where(one_one, up(here[3]), up(here[0])))
        second = jnp.where(one_last, here[0], down(here[3]))
        coupling = jnp.where(
            one_none,
            next_one[1],
            jnp.where(one_one, up(next_two[3]), jnp.where(one_last, up(next_one[0]), up(next_two[1]))),
        )
        if turn == ROUNDS - 2:
            continue
        tt, tb, bt, bb = both_sides(
            blocks,
            jnp.broadcast_to(c, shape),
            jnp.broadcast_to(s, shape),
            along_columns(c),
            along_columns(s),
        )
        column, corner = jnp.where(j_none, tb, tt), jnp.where(j_none, bb, bt)
        blocks = (
            jnp.where(
                i_none,
                jnp.where(j_none, tt, less(column)),
                jnp.where(j_none, up(more(jnp.where(i_none, bt, tt))), up(jnp.where(i_none, corner, column))),
            ),
            jnp.where(
                i_none,
                more(tb),
                jnp.where(j_last, up(more(tt)), up(more(jnp.where(i_none, bb, tb), 2))),
            ),
            jnp.where(
                i_last,
                less(tt),
                jnp.where(
                    j_none, down(less(bt)), jnp.where(j_one, down(less(bb, 2)), down(less(bt, 2)))
                ),
            ),
            jnp.where(
                i_last,
                jnp.where(j_last, tt, more(tb)),
                jnp.where(j_last, down(less(bt)), down(bb)),
            ),
        )
    return cosines, sines


def advanced(t, b):
    at = lanes(t[0].shape)
    t0, t1, b0, b1 = turn_lanes(t[0], 1), turn_lanes(t[1], 1), turn_lanes(b[0], -1), turn_lanes(b[1], -1)
    return (
        (
            jnp.where(at >= 2, t0, jnp.where(at == 1, turn_lanes(b[0], 1), t[0])),
            jnp.where(at >= 1, t1, t0),
        ),
        (jnp.where(at == 127, b1, b0), jnp.where(at == 127, t[1], b1)),
    )


MOVES = ROUNDS - 1


def retreated_top(t, b):
    at = lanes(t[0].shape)
    back = [turn_lanes(x, -MOVES) for x in t]
    from_bottom = picked(b[1], (250 - at) % 128)
    return (
        jnp.where(at == 0, t[0], jnp.where(at < 128 - MOVES, back[0], back[1])),
        jnp.where(at < 128 - MOVES, back[1], from_bottom),
    )


def retreated_bottom(t, b):
    at = lanes(t[0].shape)
    on = [turn_lanes(x, MOVES) for x in b]
    from_top = picked(t[0], (MOVES - at) % 128)
    return (
        jnp.where(at < MOVES, from_top, on[0]),
        jnp.where(at < MOVES, on[0], on[1]),
    )


def unfolded_bottom(t, b):
    at = lanes(t[0].shape)
    index = (122 - at) % 128
    low, high = picked(b[0], index), picked(b[1], index)
    return (
        jnp.where(at <= 122, high, low),
        jnp.where(at <= 122, low, turn_lanes(t[0], 122)),
    )


def turned_chunks(load, store, count, rows, cosines, sines):
    def chunk(k, carry):
        t, b = load(k)
        for turn in range(ROUNDS):
            c, s = cosines[turn], sines[turn]
            t, b = (
                tuple(c[h] * t[h] - s[h] * b[h] for h in range(2)),
                tuple(s[h] * t[h] + c[h] * b[h] for h in range(2)),
            )
            if turn < MOVES:
                t, b = advanced(t, b)
        store(k, t, b)
        return carry

    def wide(x):
        x = jnp.broadcast_to(x, (rows, HALF))
        return x[:, :128], x[:, 128:]

    cosines, sines = [wide(c) for c in cosines], [wide(s) for s in sines]
    lax.fori_loop(0, count, chunk, 0)


def rows_at(k, rows):
    return pl.ds(pl.multiple_of(k * rows, rows), rows)


CHUNK = 256


def first_band(p_ref, out_ref, b_ref, sums_ref):
    def fold(k, carry):
        at = rows_at(k, CHUNK)
        b_ref[at, :128], b_ref[at, 128:] = mirrored(p_ref[at, 256:384], p_ref[at, 384:])
        return carry

    lax.fori_loop(0, p_ref.shape[0] // CHUNK, fold, 0)

    def load(k):
        at = rows_at(k, 8)
        return halves(p_ref, at), halves(b_ref, at)

    band_of(load, p_ref.shape[0] // 8, out_ref, sums_ref)


def first_angles(parts_ref, turns_ref, x_ref):
    cosines, sines = angles_of(parts_ref, x_ref)
    turns_ref[...] = jnp.zeros_like(turns_ref)
    for k in range(ROUNDS):
        turns_ref[k : k + 1, :] = cosines[k]
        turns_ref[8 + k : 9 + k, :] = sines[k]


def given(turns_ref):
    return (
        [turns_ref[k : k + 1, :] for k in range(ROUNDS)],
        [turns_ref[8 + k : 9 + k, :] for k in range(ROUNDS)],
    )


def own_turn(turns_ref, p_ref, b_ref, t_out, top_ref):
    def load(k):
        at = rows_at(k, CHUNK)
        return halves(p_ref, at), halves(b_ref, at)

    def store(k, t, b):
        at = rows_at(k, CHUNK)
        t_out[at, :128], t_out[at, 128:] = retreated_top(t, b)

    turned_chunks(load, store, t_out.shape[0] // CHUNK, CHUNK, *given(turns_ref))
    top_band_of(lambda k: halves(t_out, rows_at(k, 8)), t_out.shape[0] // 8, top_ref)


def arrived_turn(turns_ref, p_ref, t_ref, top_ref, b_out, out_ref, sums_ref):
    def load(k):
        at = rows_at(k, CHUNK)
        return halves(p_ref, at), mirrored(p_ref[at, 256:384], p_ref[at, 384:])

    def store(k, t, b):
        at = rows_at(k, CHUNK)
        b_out[at, :128], b_out[at, 128:] = retreated_bottom(t, b)

    turned_chunks(load, store, t_ref.shape[0] // CHUNK, CHUNK, *given(turns_ref))

    def rows(k):
        at = rows_at(k, 8)
        return halves(t_ref, at), halves(b_out, at)

    band_of(rows, t_ref.shape[0] // 8, out_ref, sums_ref, top_ref)


def second_turn(parts_ref, t_ref, b_ref, out_ref, x_ref):
    cosines, sines = angles_of(parts_ref, x_ref)

    def load(k):
        at = rows_at(k, CHUNK)
        return halves(t_ref, at), halves(b_ref, at)

    def store(k, t, b):
        at = rows_at(k, CHUNK)
        out_ref[at, :128], out_ref[at, 128:256] = retreated_top(t, b)
        out_ref[at, 256:384], out_ref[at, 384:] = unfolded_bottom(t, b)

    turned_chunks(load, store, t_ref.shape[0] // CHUNK, CHUNK, cosines, sines)


def call(body, outs, args, scratch=()):
    vmem = pl.BlockSpec(memory_space=pltpu.VMEM)
    shapes = [jax.ShapeDtypeStruct(s, f32) for s in outs]
    return pl.pallas_call(
        body,
        out_shape=shapes,
        in_specs=[vmem] * len(args),
        out_specs=[vmem] * len(outs),
        scratch_shapes=[pltpu.VMEM(s, f32) for s in scratch],
        compiler_params=pltpu.CompilerParams(vmem_limit_bytes=32 * 1024 * 1024),
        interpret=INTERPRET,
    )(*args)


NEAR, FAR = "near", "far"


def exchanged(parts, near, far):
    arrived = lax.all_to_all(parts, NEAR, 0, 0, tiled=True)
    total = arrived[0]
    for k in range(1, near):
        total = total + arrived[k]
    again = jnp.broadcast_to(total[None], (far, *total.shape))
    return lax.all_to_all(again, FAR, 0, 0, tiled=True)


SUMS = [(8 * LINES + 64, 128)]
STATE = [(4, DIAGS, HALF)]


TOP = (2 * 6 * 8, 128)
TURNS = (16, HALF)


def per_device(snapshots, near, far, groups):
    rows = snapshots.shape[0]
    square, band = (rows, HALF), (near, LINES, 128)
    onward = [(i, (i + 1) % groups) for i in range(groups)]
    raw = lax.ppermute(snapshots, "grp", onward)
    parts, b = call(first_band, [band, square], [snapshots], SUMS)
    (turns,) = call(first_angles, [TURNS], [exchanged(parts, near, far)], STATE)
    their_turns = lax.ppermute(turns, "grp", onward)
    t, top = call(own_turn, [square, TOP], [turns, snapshots, b])
    b, parts = call(arrived_turn, [square, band], [their_turns, raw, t, top], SUMS)
    (out,) = call(second_turn, [(rows, 2 * HALF)], [exchanged(parts, near, far), t, b], STATE)
    return out


def solution(mesh):
    groups, rows = mesh.shape["grp"], mesh.shape["row"]
    near, far = 4, rows // 4
    fine = Mesh(mesh.devices.reshape(groups, far, near), ("grp", "far", "near"))
    placed = P(("far", "near"), "grp")
    body = functools.partial(per_device, near=near, far=far, groups=groups)
    return jax.shard_map(body, mesh=fine, in_specs=(placed,), out_specs=placed, check_vma=False)
```

```python
import jax
import jax.numpy as jnp
from jax import lax
from jax.experimental import pallas as pl
from jax.experimental.pallas import tpu as pltpu
from jax.sharding import Mesh
from jax.sharding import PartitionSpec as P

ROUNDS = 6
HALF = 256
REACH = 10
DIAGS = 24
MID = 12
WIDE = 23
LINES = 48
WINDOW = 16

f32 = jnp.float32
INTERPRET = False


def lanes(shape):
    return lax.broadcasted_iota(jnp.int32, shape, 1)


def turn_lanes(x, by):
    by %= x.shape[1]
    return pltpu.roll(x, by, axis=1) if by else x


def turn_lines(x, by):
    return pltpu.roll(x, by % x.shape[0], axis=0)


def picked(x, index):
    return jnp.take_along_axis(x, index, axis=1, mode="promise_in_bounds")


def mirrored(low, high):
    index = 127 - lanes(low.shape)
    return picked(high, index), picked(low, index)


def ends(t, b):
    at = lanes(t[0].shape)
    e = jnp.where(
        at < 16,
        t[0],
        jnp.where(at < 32, turn_lanes(t[1], 26), jnp.where(at < 48, turn_lanes(b[0], 32), turn_lanes(b[1], 58))),
    )
    swapped = jnp.where(at < 96, turn_lanes(e, 32), turn_lanes(e, 96))
    return jnp.where(at < 64, e, turn_lanes(e, 64)), jnp.where(at < 64, e, swapped)


def place_of_odd(shape):
    k = lax.broadcasted_iota(jnp.int32, shape, 0)
    return k, REACH // 2 - k, (k * (REACH + 1 - k)) // 2


def packed_odd(sums):
    k, count, start = place_of_odd(sums.shape)
    at = lanes(sums.shape)
    inside = at % WINDOW - start
    first = jnp.where((at // WINDOW) % 2 == 0, 0, REACH // 2 - 1 - k)
    index = jnp.clip(at - at % WINDOW + first + inside, 0, 127)
    used = (k < REACH // 2) & (inside >= 0) & (inside < count)
    return jnp.sum(jnp.where(used, picked(sums, index), 0.0), axis=0, keepdims=True)


def unpacked_odd(line, window, mirror):
    line = jnp.broadcast_to(line, (8, 128))
    k, count, start = place_of_odd(line.shape)
    at = lanes(line.shape) - (2 * k + 1 if mirror else 0)
    out = []
    for end in range(2):
        inside = at - (128 - REACH + REACH // 2 - 1 - k if end else 0)
        used = (k < REACH // 2) & (inside >= 0) & (inside < count)
        index = jnp.clip((window + end) * WINDOW + start + inside, 0, 127)
        out.append(jnp.where(used, picked(line, index), 0.0))
    return jnp.concatenate(out, axis=1)


def ahead(x, d):
    low, high = (turn_lanes(half, -d) for half in x)
    return jnp.where(lanes(low.shape) < 128 - d, low, high), high


def halves(ref, at):
    return ref[at, :128], ref[at, 128:256]


def over_rows(load, count, step, n):
    zeros = (jnp.zeros((8, 128), f32),) * n
    return lax.fori_loop(0, count, lambda k, sums: step(*load(k), sums), zeros, unroll=16)


def top_band_of(load, count, top_ref):
    def step(t, sums):
        new = []
        for d in range(0, REACH + 1, 2):
            shifted = ahead(t, d) if d else t
            new += [t[h] * shifted[h] for h in range(2)]
        return tuple(x + y for x, y in zip(sums, new))

    sums = over_rows(lambda k: (load(k),), count, step, 12)
    for h in range(2):
        for j in range(6):
            top_ref[pl.ds(48 * h + 8 * j, 8), :] = sums[2 * j + h]


def band_of(load, count, out_ref, sums_ref, top_ref=None):
    def with_top(t, b, sums):
        new = []
        for d in range(2 if top_ref is not None else 0, REACH + 1, 2):
            shifted = ahead(t, d) if d else t
            if top_ref is None:
                new += [t[h] * shifted[h] for h in range(2)]
            if d:
                new += [b[h] * shifted[h] for h in range(2)]
        return tuple(x + y for x, y in zip(sums, new))

    def with_bottom(t, b, sums):
        new = []
        for d in range(0, REACH + 1, 2):
            shifted = ahead(b, d) if d else b
            for left in (b, t):
                new += [left[h] * shifted[h] for h in range(2)]
        return tuple(x + y for x, y in zip(sums, new))

    def at_ends(t, b, sums):
        left, right = ends(t, b)
        new = [left * turn_lanes(right, -d) for d in range(1, REACH, 2)]
        return tuple(x + y for x, y in zip(sums, new))

    def keep(line, value):
        sums_ref[pl.ds(8 * line, 8), :] = value

    if top_ref is not None:
        sums = over_rows(load, count, with_top, 10)
        for h in range(2):
            sums_ref[pl.ds(8 * 24 * h, 48), :] = top_ref[pl.ds(48 * h, 48), :]
            for j in range(1, 6):
                keep(24 * h + 17 + j, sums[2 * j - 2 + h])
    else:
        sums = over_rows(load, count, with_top, 22)
        for h in range(2):
            keep(24 * h, sums[h])
            for j in range(1, 6):
                keep(24 * h + j, sums[4 * j - 2 + h])
                keep(24 * h + 17 + j, sums[4 * j + h])
    sums = over_rows(load, count, with_bottom, 24)
    for h in range(2):
        for j in range(6):
            keep(24 * h + 6 + j, sums[4 * j + h])
            keep(24 * h + 12 + j, sums[4 * j + 2 + h])
    sums = over_rows(load, count, at_ends, 5)
    for j in range(5):
        keep(LINES + j, sums[j])
    for line in (WIDE, LINES - 1, LINES + 5, LINES + 6, LINES + 7):
        keep(line, jnp.zeros((8, 128), f32))
    parts = [sums_ref[pl.ds(k, LINES + 8, stride=8), :] for k in range(8)]
    while len(parts) > 1:
        parts = [x + y for x, y in zip(parts[::2], parts[1::2])]
    odd = packed_odd(parts[0][LINES:])
    for k in range(out_ref.shape[0]):
        out_ref[k] = parts[0][:LINES]
        out_ref[k, WIDE : WIDE + 1, :] = odd


def along_columns(x):
    shifted = jnp.broadcast_to(turn_lanes(x, -MID), (DIAGS, HALF))
    return pltpu.roll(shifted, 0, axis=1, stride=1, stride_axis=0)


def angles_of(parts_ref, x_ref):
    band = parts_ref[0]
    for k in range(1, parts_ref.shape[0]):
        band = band + parts_ref[k]
    low, high = band[:24], band[24:]
    blank = jnp.zeros((1, HALF), f32)
    for block in range(4):
        for line in (0, DIAGS - 2, DIAGS - 1):
            x_ref[block, line : line + 1, :] = blank
    TT, TB, BT, BB = 0, 1, 2, 3

    def put(block, other, d, value):
        x_ref[block, MID - d : MID - d + 1, :] = value
        x_ref[other, MID + d : MID + d + 1, :] = turn_lanes(value, d)

    def line(k):
        return jnp.concatenate([low[k : k + 1], high[k : k + 1]], axis=1)

    for j in range(6):
        put(TT, TT, 2 * j, line(j))
        put(BB, BB, 2 * j, line(6 + j))
        put(TB, BT, 2 * j, line(12 + j))
        if j:
            put(BT, TB, 2 * j, line(17 + j))
    for window, (block, other) in enumerate(((TT, TT), (BB, BB), (TB, BT), (BT, TB))):
        there = unpacked_odd(low[WIDE : WIDE + 1], 2 * window, False)
        mirror = unpacked_odd(low[WIDE : WIDE + 1], 2 * window, True)
        for j in range(5):
            d = 2 * j + 1
            x_ref[block, MID - d : MID - d + 1, :] = there[j : j + 1]
            x_ref[other, MID + d : MID + d + 1, :] = mirror[j : j + 1]

    tt, tb, bt, bb = (x_ref[k] for k in range(4))
    shape = (DIAGS, HALF)
    i = lanes(shape)
    j = i + MID - lax.broadcasted_iota(jnp.int32, shape, 0)
    i_none, i_one, i_last = i == 0, i == 1, i == HALF - 1
    j_none, j_one, j_last = j == 0, j == 1, j == HALF - 1
    one = lanes((1, HALF))
    one_none, one_one, one_last = one == 0, one == 1, one == HALF - 1

    def less(x, by=1):
        return turn_lines(x, -by)

    def more(x, by=1):
        return turn_lines(x, by)

    def up(x):
        return turn_lanes(x, 1)

    def down(x):
        return turn_lanes(x, -1)

    def both_sides(blocks, c_row, s_row, c_col, s_col):
        tt, tb, bt, bb = blocks
        tt, tb = c_col * tt - s_col * tb, s_col * tt + c_col * tb
        bt, bb = c_col * bt - s_col * bb, s_col * bt + c_col * bb
        tt, bt = c_row * tt - s_row * bt, s_row * tt + c_row * bt
        tb, bb = c_row * tb - s_row * bb, s_row * tb + c_row * bb
        return tt, tb, bt, bb

    cosines, sines = [], []
    blocks = tt, tb, bt, bb
    first, second, coupling = (x[MID : MID + 1] for x in (tt, bb, tb))
    for turn in range(ROUNDS):
        difference = second - first
        direction = jnp.where(difference >= 0, 1.0, -1.0)
        denominator = (
            jnp.abs(difference)
            + jnp.sqrt(difference * difference + 4.0 * coupling * coupling)
            + 1e-06 * (first + second)
        )
        tangent = direction * 2.0 * coupling / denominator
        c = lax.rsqrt(1.0 + tangent * tangent)
        s = tangent * c
        cosines.append(c)
        sines.append(s)
        if turn == ROUNDS - 1:
            break
        here = both_sides([x[MID : MID + 1] for x in blocks], c, s, c, s)
        next_one = both_sides([x[MID - 1 : MID] for x in blocks], c, s, down(c), down(s))
        next_two = both_sides([x[MID - 2 : MID - 1] for x in blocks], c, s, turn_lanes(c, -2), turn_lanes(s, -2))
        first = jnp.where(one_none, here[0], jnp.where(one_one, up(here[3]), up(here[0])))
        second = jnp.where(one_last, here[0], down(here[3]))
        coupling = jnp.where(
            one_none,
            next_one[1],
            jnp.where(one_one, up(next_two[3]), jnp.where(one_last, up(next_one[0]), up(next_two[1]))),
        )
        if turn == ROUNDS - 2:
            continue
        tt, tb, bt, bb = both_sides(
            blocks,
            jnp.broadcast_to(c, shape),
            jnp.broadcast_to(s, shape),
            along_columns(c),
            along_columns(s),
        )
        column, corner = jnp.where(j_none, tb, tt), jnp.where(j_none, bb, bt)
        blocks = (
            jnp.where(
                i_none,
                jnp.where(j_none, tt, less(column)),
                jnp.where(j_none, up(more(jnp.where(i_none, bt, tt))), up(jnp.where(i_none, corner, column))),
            ),
            jnp.where(
                i_none,
                more(tb),
                jnp.where(j_last, up(more(tt)), up(more(jnp.where(i_none, bb, tb), 2))),
            ),
            jnp.where(
                i_last,
                less(tt),
                jnp.where(
                    j_none, down(less(bt)), jnp.where(j_one, down(less(bb, 2)), down(less(bt, 2)))
                ),
            ),
            jnp.where(
                i_last,
                jnp.where(j_last, tt, more(tb)),
                jnp.where(j_last, down(less(bt)), down(bb)),
            ),
        )
    return cosines, sines


def advanced(t, b):
    at = lanes(t[0].shape)
    t0, t1, b0, b1 = turn_lanes(t[0], 1), turn_lanes(t[1], 1), turn_lanes(b[0], -1), turn_lanes(b[1], -1)
    return (
        (
            jnp.where(at >= 2, t0, jnp.where(at == 1, turn_lanes(b[0], 1), t[0])),
            jnp.where(at >= 1, t1, t0),
        ),
        (jnp.where(at == 127, b1, b0), jnp.where(at == 127, t[1], b1)),
    )


MOVES = ROUNDS - 1


def retreated_top(t, b):
    at = lanes(t[0].shape)
    back = [turn_lanes(x, -MOVES) for x in t]
    from_bottom = picked(b[1], (250 - at) % 128)
    return (
        jnp.where(at == 0, t[0], jnp.where(at < 128 - MOVES, back[0], back[1])),
        jnp.where(at < 128 - MOVES, back[1], from_bottom),
    )


def retreated_bottom(t, b):
    at = lanes(t[0].shape)
    on = [turn_lanes(x, MOVES) for x in b]
    from_top = picked(t[0], (MOVES - at) % 128)
    return (
        jnp.where(at < MOVES, from_top, on[0]),
        jnp.where(at < MOVES, on[0], on[1]),
    )


def unfolded_bottom(t, b):
    at = lanes(t[0].shape)
    index = (122 - at) % 128
    low, high = picked(b[0], index), picked(b[1], index)
    return (
        jnp.where(at <= 122, high, low),
        jnp.where(at <= 122, low, turn_lanes(t[0], 122)),
    )


def turned_chunks(load, store, count, rows, cosines, sines):
    def chunk(k, carry):
        t, b = load(k)
        for turn in range(ROUNDS):
            c, s = cosines[turn], sines[turn]
            t, b = (
                tuple(c[h] * t[h] - s[h] * b[h] for h in range(2)),
                tuple(s[h] * t[h] + c[h] * b[h] for h in range(2)),
            )
            if turn < MOVES:
                t, b = advanced(t, b)
        store(k, t, b)
        return carry

    def wide(x):
        x = jnp.broadcast_to(x, (rows, HALF))
        return x[:, :128], x[:, 128:]

    cosines, sines = [wide(c) for c in cosines], [wide(s) for s in sines]
    lax.fori_loop(0, count, chunk, 0)


def rows_at(k, rows):
    return pl.ds(pl.multiple_of(k * rows, rows), rows)


CHUNK = 256


def first_band(p_ref, out_ref, b_ref, sums_ref):
    def fold(k, carry):
        at = rows_at(k, CHUNK)
        b_ref[at, :128], b_ref[at, 128:] = mirrored(p_ref[at, 256:384], p_ref[at, 384:])
        return carry

    lax.fori_loop(0, p_ref.shape[0] // CHUNK, fold, 0)

    def load(k):
        at = rows_at(k, 8)
        return halves(p_ref, at), halves(b_ref, at)

    band_of(load, p_ref.shape[0] // 8, out_ref, sums_ref)


def first_angles(parts_ref, turns_ref, x_ref):
    cosines, sines = angles_of(parts_ref, x_ref)
    turns_ref[...] = jnp.zeros_like(turns_ref)
    for k in range(ROUNDS):
        turns_ref[k : k + 1, :] = cosines[k]
        turns_ref[8 + k : 9 + k, :] = sines[k]


def given(turns_ref):
    return (
        [turns_ref[k : k + 1, :] for k in range(ROUNDS)],
        [turns_ref[8 + k : 9 + k, :] for k in range(ROUNDS)],
    )


def own_turn(turns_ref, p_ref, b_ref, t_out, top_ref):
    def load(k):
        at = rows_at(k, CHUNK)
        return halves(p_ref, at), halves(b_ref, at)

    def store(k, t, b):
        at = rows_at(k, CHUNK)
        t_out[at, :128], t_out[at, 128:] = retreated_top(t, b)

    turned_chunks(load, store, t_out.shape[0] // CHUNK, CHUNK, *given(turns_ref))
    top_band_of(lambda k: halves(t_out, rows_at(k, 8)), t_out.shape[0] // 8, top_ref)


def arrived_turn(turns_ref, p_ref, t_ref, top_ref, b_out, out_ref, sums_ref):
    def load(k):
        at = rows_at(k, CHUNK)
        return halves(p_ref, at), mirrored(p_ref[at, 256:384], p_ref[at, 384:])

    def store(k, t, b):
        at = rows_at(k, CHUNK)
        b_out[at, :128], b_out[at, 128:] = retreated_bottom(t, b)

    turned_chunks(load, store, t_ref.shape[0] // CHUNK, CHUNK, *given(turns_ref))

    def rows(k):
        at = rows_at(k, 8)
        return halves(t_ref, at), halves(b_out, at)

    band_of(rows, t_ref.shape[0] // 8, out_ref, sums_ref, top_ref)


def second_turn(parts_ref, t_ref, b_ref, out_ref, x_ref):
    cosines, sines = angles_of(parts_ref, x_ref)

    def load(k):
        at = rows_at(k, CHUNK)
        return halves(t_ref, at), halves(b_ref, at)

    def store(k, t, b):
        at = rows_at(k, CHUNK)
        out_ref[at, :128], out_ref[at, 128:256] = retreated_top(t, b)
        out_ref[at, 256:384], out_ref[at, 384:] = unfolded_bottom(t, b)

    turned_chunks(load, store, t_ref.shape[0] // CHUNK, CHUNK, cosines, sines)


def call(body, outs, args, scratch=()):
    vmem = pl.BlockSpec(memory_space=pltpu.VMEM)
    shapes = [jax.ShapeDtypeStruct(s, f32) for s in outs]
    return pl.pallas_call(
        body,
        out_shape=shapes,
        in_specs=[vmem] * len(args),
        out_specs=[vmem] * len(outs),
        scratch_shapes=[pltpu.VMEM(s, f32) for s in scratch],
        compiler_params=pltpu.CompilerParams(vmem_limit_bytes=32 * 1024 * 1024),
        interpret=INTERPRET,
    )(*args)


ROW_AXES = ("z3", "z2", "z1", "z0", "side")
FIRST_SUM = (("z1", "z0", "side"), ("z3", "z2"))
SECOND_SUM = (("z0", "side"), ("z3", "z2", "z1"))


def exchanged(parts, stages):
    near, far = stages
    arrived = lax.all_to_all(parts, near, 0, 0, tiled=True)
    total = arrived[0]
    for k in range(1, arrived.shape[0]):
        total = total + arrived[k]
    again = jnp.broadcast_to(total[None], (lax.axis_size(far), *total.shape))
    return lax.all_to_all(again, far, 0, 0, tiled=True)


SUMS = [(8 * LINES + 64, 128)]
STATE = [(4, DIAGS, HALF)]


TOP = (2 * 6 * 8, 128)
TURNS = (16, HALF)


def per_device(snapshots):
    rows = snapshots.shape[0]
    square = (rows, HALF)
    first, second = ((lax.axis_size(stages[0]), LINES, 128) for stages in (FIRST_SUM, SECOND_SUM))
    groups = lax.axis_size("grp")
    onward = [(i, (i + 1) % groups) for i in range(groups)]
    raw = lax.ppermute(snapshots, "grp", onward)
    parts, b = call(first_band, [first, square], [snapshots], SUMS)
    (turns,) = call(first_angles, [TURNS], [exchanged(parts, FIRST_SUM)], STATE)
    their_turns = lax.ppermute(turns, "grp", onward)
    t, top = call(own_turn, [square, TOP], [turns, snapshots, b])
    b, parts = call(arrived_turn, [square, second], [their_turns, raw, t, top], SUMS)
    (out,) = call(second_turn, [(rows, 2 * HALF)], [exchanged(parts, SECOND_SUM), t, b], STATE)
    return out


def solution(mesh):
    sizes = (mesh.shape["grp"], mesh.shape["row"] // 16, 2, 2, 2, 2)
    fine = Mesh(mesh.devices.reshape(sizes), ("grp", *ROW_AXES))
    placed = P(ROW_AXES, "grp")
    return jax.shard_map(per_device, mesh=fine, in_specs=(placed,), out_specs=placed, check_vma=False)
```

```python
import jax
import jax.numpy as jnp
from jax import lax
from jax.experimental import pallas as pl
from jax.experimental.pallas import tpu as pltpu
from jax.sharding import Mesh
from jax.sharding import PartitionSpec as P

ROUNDS = 6
HALF = 256
REACH = 10
DIAGS = 24
MID = 12
WIDE = 23
LINES = 48
WINDOW = 16

f32 = jnp.float32
INTERPRET = False


def lanes(shape):
    return lax.broadcasted_iota(jnp.int32, shape, 1)


def turn_lanes(x, by):
    by %= x.shape[1]
    return pltpu.roll(x, by, axis=1) if by else x


def turn_lines(x, by):
    return pltpu.roll(x, by % x.shape[0], axis=0)


def picked(x, index):
    return jnp.take_along_axis(x, index, axis=1, mode="promise_in_bounds")


def mirrored(low, high):
    index = 127 - lanes(low.shape)
    return picked(high, index), picked(low, index)


def ends(t, b):
    at = lanes(t[0].shape)
    e = jnp.where(
        at < 16,
        t[0],
        jnp.where(at < 32, turn_lanes(t[1], 26), jnp.where(at < 48, turn_lanes(b[0], 32), turn_lanes(b[1], 58))),
    )
    swapped = jnp.where(at < 96, turn_lanes(e, 32), turn_lanes(e, 96))
    return jnp.where(at < 64, e, turn_lanes(e, 64)), jnp.where(at < 64, e, swapped)


def place_of_odd(shape):
    k = lax.broadcasted_iota(jnp.int32, shape, 0)
    return k, REACH // 2 - k, (k * (REACH + 1 - k)) // 2


def packed_odd(sums):
    k, count, start = place_of_odd(sums.shape)
    at = lanes(sums.shape)
    inside = at % WINDOW - start
    first = jnp.where((at // WINDOW) % 2 == 0, 0, REACH // 2 - 1 - k)
    index = jnp.clip(at - at % WINDOW + first + inside, 0, 127)
    used = (k < REACH // 2) & (inside >= 0) & (inside < count)
    return jnp.sum(jnp.where(used, picked(sums, index), 0.0), axis=0, keepdims=True)


def unpacked_odd(line, window, mirror):
    line = jnp.broadcast_to(line, (8, 128))
    k, count, start = place_of_odd(line.shape)
    at = lanes(line.shape) - (2 * k + 1 if mirror else 0)
    out = []
    for end in range(2):
        inside = at - (128 - REACH + REACH // 2 - 1 - k if end else 0)
        used = (k < REACH // 2) & (inside >= 0) & (inside < count)
        index = jnp.clip((window + end) * WINDOW + start + inside, 0, 127)
        out.append(jnp.where(used, picked(line, index), 0.0))
    return jnp.concatenate(out, axis=1)


def ahead(x, d):
    low, high = (turn_lanes(half, -d) for half in x)
    return jnp.where(lanes(low.shape) < 128 - d, low, high), high


def halves(ref, at):
    return ref[at, :128], ref[at, 128:256]


def over_rows(load, count, step, n):
    zeros = (jnp.zeros((8, 128), f32),) * n
    return lax.fori_loop(0, count, lambda k, sums: step(*load(k), sums), zeros, unroll=16)


def top_band_of(load, count, top_ref):
    def step(t, sums):
        new = []
        for d in range(0, REACH + 1, 2):
            shifted = ahead(t, d) if d else t
            new += [t[h] * shifted[h] for h in range(2)]
        return tuple(x + y for x, y in zip(sums, new))

    sums = over_rows(lambda k: (load(k),), count, step, 12)
    for h in range(2):
        for j in range(6):
            top_ref[pl.ds(48 * h + 8 * j, 8), :] = sums[2 * j + h]


def band_of(load, count, out_ref, sums_ref, top_ref=None):
    def with_top(t, b, sums):
        new = []
        for d in range(2 if top_ref is not None else 0, REACH + 1, 2):
            shifted = ahead(t, d) if d else t
            if top_ref is None:
                new += [t[h] * shifted[h] for h in range(2)]
            if d:
                new += [b[h] * shifted[h] for h in range(2)]
        return tuple(x + y for x, y in zip(sums, new))

    def with_bottom(t, b, sums):
        new = []
        for d in range(0, REACH + 1, 2):
            shifted = ahead(b, d) if d else b
            for left in (b, t):
                new += [left[h] * shifted[h] for h in range(2)]
        return tuple(x + y for x, y in zip(sums, new))

    def at_ends(t, b, sums):
        left, right = ends(t, b)
        new = [left * turn_lanes(right, -d) for d in range(1, REACH, 2)]
        return tuple(x + y for x, y in zip(sums, new))

    def with_top_and_ends(t, b, sums):
        return with_top(t, b, sums[:-5]) + at_ends(t, b, sums[-5:])

    def keep(line, value):
        sums_ref[pl.ds(8 * line, 8), :] = value

    if top_ref is not None:
        sums = over_rows(load, count, with_top_and_ends, 15)
        for h in range(2):
            sums_ref[pl.ds(8 * 24 * h, 48), :] = top_ref[pl.ds(48 * h, 48), :]
            for j in range(1, 6):
                keep(24 * h + 17 + j, sums[2 * j - 2 + h])
    else:
        sums = over_rows(load, count, with_top_and_ends, 27)
        for h in range(2):
            keep(24 * h, sums[h])
            for j in range(1, 6):
                keep(24 * h + j, sums[4 * j - 2 + h])
                keep(24 * h + 17 + j, sums[4 * j + h])
    odd_sums = sums[-5:]
    sums = over_rows(load, count, with_bottom, 24)
    for h in range(2):
        for j in range(6):
            keep(24 * h + 6 + j, sums[4 * j + h])
            keep(24 * h + 12 + j, sums[4 * j + 2 + h])
    for j in range(5):
        keep(LINES + j, odd_sums[j])
    for line in (WIDE, LINES - 1, LINES + 5, LINES + 6, LINES + 7):
        keep(line, jnp.zeros((8, 128), f32))
    parts = [sums_ref[pl.ds(k, LINES + 8, stride=8), :] for k in range(8)]
    while len(parts) > 1:
        parts = [x + y for x, y in zip(parts[::2], parts[1::2])]
    odd = packed_odd(parts[0][LINES:])
    for k in range(out_ref.shape[0]):
        out_ref[k] = parts[0][:LINES]
        out_ref[k, WIDE : WIDE + 1, :] = odd


def along_columns(x):
    shifted = jnp.broadcast_to(turn_lanes(x, -MID), (DIAGS, HALF))
    return pltpu.roll(shifted, 0, axis=1, stride=1, stride_axis=0)


def angles_of(parts_ref, x_ref):
    band = parts_ref[0]
    for k in range(1, parts_ref.shape[0]):
        band = band + parts_ref[k]
    low, high = band[:24], band[24:]
    blank = jnp.zeros((1, HALF), f32)
    for block in range(4):
        for line in (0, 1, DIAGS - 1):
            x_ref[block, line : line + 1, :] = blank
    TT, TB, BT, BB = 0, 1, 2, 3

    def put(block, other, d, value):
        x_ref[block, MID - d : MID - d + 1, :] = value
        x_ref[other, MID + d : MID + d + 1, :] = turn_lanes(value, d)

    def line(k):
        return jnp.concatenate([low[k : k + 1], high[k : k + 1]], axis=1)

    for j in range(6):
        put(TT, TT, 2 * j, line(j))
        put(BB, BB, 2 * j, line(6 + j))
        put(TB, BT, 2 * j, line(12 + j))
        if j:
            put(BT, TB, 2 * j, line(17 + j))
    for window, (block, other) in enumerate(((TT, TT), (BB, BB), (TB, BT), (BT, TB))):
        there = unpacked_odd(low[WIDE : WIDE + 1], 2 * window, False)
        mirror = unpacked_odd(low[WIDE : WIDE + 1], 2 * window, True)
        for j in range(5):
            d = 2 * j + 1
            x_ref[block, MID - d : MID - d + 1, :] = there[j : j + 1]
            x_ref[other, MID + d : MID + d + 1, :] = mirror[j : j + 1]

    tt, tb, bt, bb = (x_ref[k] for k in range(4))
    shape = (DIAGS, HALF)
    i = lanes(shape)
    j = i + MID - lax.broadcasted_iota(jnp.int32, shape, 0)
    i_none, i_one, i_last = i == 0, i == 1, i == HALF - 1
    j_none, j_one, j_last = j == 0, j == 1, j == HALF - 1
    one = lanes((1, HALF))
    one_none, one_one, one_last = one == 0, one == 1, one == HALF - 1

    def less(x, by=1):
        return turn_lines(x, -by)

    def more(x, by=1):
        return turn_lines(x, by)

    def up(x):
        return turn_lanes(x, 1)

    def down(x):
        return turn_lanes(x, -1)

    def both_sides(blocks, c_row, s_row, c_col, s_col):
        tt, tb, bt, bb = blocks
        tt, tb = c_col * tt - s_col * tb, s_col * tt + c_col * tb
        bt, bb = c_col * bt - s_col * bb, s_col * bt + c_col * bb
        tt, bt = c_row * tt - s_row * bt, s_row * tt + c_row * bt
        tb, bb = c_row * tb - s_row * bb, s_row * tb + c_row * bb
        return tt, tb, bt, bb

    cosines, sines = [], []
    blocks = tt, tb, bt, bb
    first, second, coupling = (x[MID : MID + 1] for x in (tt, bb, tb))
    for turn in range(ROUNDS):
        difference = second - first
        direction = jnp.where(difference >= 0, 1.0, -1.0)
        denominator = (
            jnp.abs(difference)
            + jnp.sqrt(difference * difference + 4.0 * coupling * coupling)
            + 1e-06 * (first + second)
        )
        tangent = direction * 2.0 * coupling / denominator
        c = lax.rsqrt(1.0 + tangent * tangent)
        s = tangent * c
        cosines.append(c)
        sines.append(s)
        if turn == ROUNDS - 1:
            break
        here = both_sides([x[MID : MID + 1] for x in blocks], c, s, c, s)
        next_one = both_sides([x[MID - 1 : MID] for x in blocks], c, s, down(c), down(s))
        next_two = both_sides([x[MID - 2 : MID - 1] for x in blocks], c, s, turn_lanes(c, -2), turn_lanes(s, -2))
        first = jnp.where(one_none, here[0], jnp.where(one_one, up(here[3]), up(here[0])))
        second = jnp.where(one_last, here[0], down(here[3]))
        coupling = jnp.where(
            one_none,
            next_one[1],
            jnp.where(one_one, up(next_two[3]), jnp.where(one_last, up(next_one[0]), up(next_two[1]))),
        )
        if turn == ROUNDS - 2:
            continue
        tt, tb, bt, bb = both_sides(
            blocks,
            jnp.broadcast_to(c, shape),
            jnp.broadcast_to(s, shape),
            along_columns(c),
            along_columns(s),
        )
        column, corner = jnp.where(j_none, tb, tt), jnp.where(j_none, bb, bt)
        blocks = (
            jnp.where(
                i_none,
                jnp.where(j_none, tt, less(column)),
                jnp.where(j_none, up(more(jnp.where(i_none, bt, tt))), up(jnp.where(i_none, corner, column))),
            ),
            jnp.where(
                i_none,
                more(tb),
                jnp.where(j_last, up(more(tt)), up(more(jnp.where(i_none, bb, tb), 2))),
            ),
            jnp.where(
                i_last,
                less(tt),
                jnp.where(
                    j_none, down(less(bt)), jnp.where(j_one, down(less(bb, 2)), down(less(bt, 2)))
                ),
            ),
            jnp.where(
                i_last,
                jnp.where(j_last, tt, more(tb)),
                jnp.where(j_last, down(less(bt)), down(bb)),
            ),
        )
    return cosines, sines


def advanced(t, b):
    at = lanes(t[0].shape)
    t0, t1, b0, b1 = turn_lanes(t[0], 1), turn_lanes(t[1], 1), turn_lanes(b[0], -1), turn_lanes(b[1], -1)
    return (
        (
            jnp.where(at >= 2, t0, jnp.where(at == 1, turn_lanes(b[0], 1), t[0])),
            jnp.where(at >= 1, t1, t0),
        ),
        (jnp.where(at == 127, b1, b0), jnp.where(at == 127, t[1], b1)),
    )


MOVES = ROUNDS - 1


def retreated_top(t, b):
    at = lanes(t[0].shape)
    back = [turn_lanes(x, -MOVES) for x in t]
    from_bottom = picked(b[1], (250 - at) % 128)
    return (
        jnp.where(at == 0, t[0], jnp.where(at < 128 - MOVES, back[0], back[1])),
        jnp.where(at < 128 - MOVES, back[1], from_bottom),
    )


def retreated_bottom(t, b):
    at = lanes(t[0].shape)
    on = [turn_lanes(x, MOVES) for x in b]
    from_top = picked(t[0], (MOVES - at) % 128)
    return (
        jnp.where(at < MOVES, from_top, on[0]),
        jnp.where(at < MOVES, on[0], on[1]),
    )


def unfolded_bottom(t, b):
    at = lanes(t[0].shape)
    index = (122 - at) % 128
    low, high = picked(b[0], index), picked(b[1], index)
    return (
        jnp.where(at <= 122, high, low),
        jnp.where(at <= 122, low, turn_lanes(t[0], 122)),
    )


def turned_chunks(load, store, count, rows, cosines, sines):
    def chunk(k, carry):
        t, b = load(k)
        for turn in range(ROUNDS):
            c, s = cosines[turn], sines[turn]
            t, b = (
                tuple(c[h] * t[h] - s[h] * b[h] for h in range(2)),
                tuple(s[h] * t[h] + c[h] * b[h] for h in range(2)),
            )
            if turn < MOVES:
                t, b = advanced(t, b)
        store(k, t, b)
        return carry

    def wide(x):
        x = jnp.broadcast_to(x, (rows, HALF))
        return x[:, :128], x[:, 128:]

    cosines, sines = [wide(c) for c in cosines], [wide(s) for s in sines]
    lax.fori_loop(0, count, chunk, 0)


def rows_at(k, rows):
    return pl.ds(pl.multiple_of(k * rows, rows), rows)


CHUNK = 256


def first_band(p_ref, out_ref, b_ref, sums_ref):
    def fold(k, carry):
        at = rows_at(k, CHUNK)
        b_ref[at, :128], b_ref[at, 128:] = mirrored(p_ref[at, 256:384], p_ref[at, 384:])
        return carry

    lax.fori_loop(0, p_ref.shape[0] // CHUNK, fold, 0)

    def load(k):
        at = rows_at(k, 8)
        return halves(p_ref, at), halves(b_ref, at)

    band_of(load, p_ref.shape[0] // 8, out_ref, sums_ref)


def first_angles(parts_ref, turns_ref, x_ref):
    cosines, sines = angles_of(parts_ref, x_ref)
    turns_ref[...] = jnp.zeros_like(turns_ref)
    for k in range(ROUNDS):
        turns_ref[k : k + 1, :] = cosines[k]
        turns_ref[8 + k : 9 + k, :] = sines[k]


def given(turns_ref):
    return (
        [turns_ref[k : k + 1, :] for k in range(ROUNDS)],
        [turns_ref[8 + k : 9 + k, :] for k in range(ROUNDS)],
    )


def own_turn(turns_ref, p_ref, b_ref, t_out, top_ref):
    def load(k):
        at = rows_at(k, CHUNK)
        return halves(p_ref, at), halves(b_ref, at)

    def store(k, t, b):
        at = rows_at(k, CHUNK)
        t_out[at, :128], t_out[at, 128:] = retreated_top(t, b)

    turned_chunks(load, store, t_out.shape[0] // CHUNK, CHUNK, *given(turns_ref))
    top_band_of(lambda k: halves(t_out, rows_at(k, 8)), t_out.shape[0] // 8, top_ref)


def arrived_turn(turns_ref, p_ref, t_ref, top_ref, b_out, out_ref, sums_ref):
    def load(k):
        at = rows_at(k, CHUNK)
        return halves(p_ref, at), mirrored(p_ref[at, 256:384], p_ref[at, 384:])

    def store(k, t, b):
        at = rows_at(k, CHUNK)
        b_out[at, :128], b_out[at, 128:] = retreated_bottom(t, b)

    turned_chunks(load, store, t_ref.shape[0] // CHUNK, CHUNK, *given(turns_ref))

    def rows(k):
        at = rows_at(k, 8)
        return halves(t_ref, at), halves(b_out, at)

    band_of(rows, t_ref.shape[0] // 8, out_ref, sums_ref, top_ref)


def second_turn(parts_ref, t_ref, b_ref, out_ref, x_ref):
    cosines, sines = angles_of(parts_ref, x_ref)

    def load(k):
        at = rows_at(k, CHUNK)
        return halves(t_ref, at), halves(b_ref, at)

    def store(k, t, b):
        at = rows_at(k, CHUNK)
        out_ref[at, :128], out_ref[at, 128:256] = retreated_top(t, b)
        out_ref[at, 256:384], out_ref[at, 384:] = unfolded_bottom(t, b)

    turned_chunks(load, store, t_ref.shape[0] // CHUNK, CHUNK, cosines, sines)


def call(body, outs, args, scratch=()):
    vmem = pl.BlockSpec(memory_space=pltpu.VMEM)
    shapes = [jax.ShapeDtypeStruct(s, f32) for s in outs]
    return pl.pallas_call(
        body,
        out_shape=shapes,
        in_specs=[vmem] * len(args),
        out_specs=[vmem] * len(outs),
        scratch_shapes=[pltpu.VMEM(s, f32) for s in scratch],
        compiler_params=pltpu.CompilerParams(vmem_limit_bytes=32 * 1024 * 1024),
        interpret=INTERPRET,
    )(*args)


ROW_AXES = ("z3", "z2", "z1", "z0", "side")
FIRST_SUM = (("z1", "z0", "side"), ("z3", "z2"))
SECOND_SUM = (("z0", "side"), ("z3", "z2", "z1"))


def exchanged(parts, stages):
    near, far = stages
    arrived = lax.all_to_all(parts, near, 0, 0, tiled=True)
    total = arrived[0]
    for k in range(1, arrived.shape[0]):
        total = total + arrived[k]
    again = jnp.broadcast_to(total[None], (lax.axis_size(far), *total.shape))
    return lax.all_to_all(again, far, 0, 0, tiled=True)


SUMS = [(8 * LINES + 64, 128)]
STATE = [(4, DIAGS, HALF)]


TOP = (2 * 6 * 8, 128)
TURNS = (16, HALF)


def per_device(snapshots):
    rows = snapshots.shape[0]
    square = (rows, HALF)
    first, second = ((lax.axis_size(stages[0]), LINES, 128) for stages in (FIRST_SUM, SECOND_SUM))
    groups = lax.axis_size("grp")
    onward = [(i, (i + 1) % groups) for i in range(groups)]
    raw = lax.ppermute(snapshots, "grp", onward)
    parts, b = call(first_band, [first, square], [snapshots], SUMS)
    (turns,) = call(first_angles, [TURNS], [exchanged(parts, FIRST_SUM)], STATE)
    their_turns = lax.ppermute(turns, "grp", onward)
    t, top = call(own_turn, [square, TOP], [turns, snapshots, b])
    b, parts = call(arrived_turn, [square, second], [their_turns, raw, t, top], SUMS)
    (out,) = call(second_turn, [(rows, 2 * HALF)], [exchanged(parts, SECOND_SUM), t, b], STATE)
    return out


def solution(mesh):
    sizes = (mesh.shape["grp"], mesh.shape["row"] // 16, 2, 2, 2, 2)
    fine = Mesh(mesh.devices.reshape(sizes), ("grp", *ROW_AXES))
    placed = P(ROW_AXES, "grp")
    return jax.shard_map(per_device, mesh=fine, in_specs=(placed,), out_specs=placed, check_vma=False)
```

```python
import jax
import jax.numpy as jnp
from jax import lax
from jax.experimental import pallas as pl
from jax.experimental.pallas import tpu as pltpu
from jax.sharding import Mesh
from jax.sharding import PartitionSpec as P

ROUNDS = 6
HALF = 256
REACH = 10
DIAGS = 24
MID = 12
WIDE = 23
LINES = 48
WINDOW = 16

f32 = jnp.float32
INTERPRET = False


def lanes(shape):
    return lax.broadcasted_iota(jnp.int32, shape, 1)


def turn_lanes(x, by):
    by %= x.shape[1]
    return pltpu.roll(x, by, axis=1) if by else x


def turn_lines(x, by):
    return pltpu.roll(x, by % x.shape[0], axis=0)


def picked(x, index):
    return jnp.take_along_axis(x, index, axis=1, mode="promise_in_bounds")


def mirrored(low, high):
    index = 127 - lanes(low.shape)
    return picked(high, index), picked(low, index)


def ends(t, b):
    at = lanes(t[0].shape)
    e = jnp.where(
        at < 16,
        t[0],
        jnp.where(at < 32, turn_lanes(t[1], 26), jnp.where(at < 48, turn_lanes(b[0], 32), turn_lanes(b[1], 58))),
    )
    swapped = jnp.where(at < 96, turn_lanes(e, 32), turn_lanes(e, 96))
    return jnp.where(at < 64, e, turn_lanes(e, 64)), jnp.where(at < 64, e, swapped)


def place_of_odd(shape):
    k = lax.broadcasted_iota(jnp.int32, shape, 0)
    return k, REACH // 2 - k, (k * (REACH + 1 - k)) // 2


def packed_odd(sums):
    k, count, start = place_of_odd(sums.shape)
    at = lanes(sums.shape)
    inside = at % WINDOW - start
    first = jnp.where((at // WINDOW) % 2 == 0, 0, REACH // 2 - 1 - k)
    index = jnp.clip(at - at % WINDOW + first + inside, 0, 127)
    used = (k < REACH // 2) & (inside >= 0) & (inside < count)
    return jnp.sum(jnp.where(used, picked(sums, index), 0.0), axis=0, keepdims=True)


def unpacked_odd(line, window, mirror):
    line = jnp.broadcast_to(line, (8, 128))
    k, count, start = place_of_odd(line.shape)
    at = lanes(line.shape) - (2 * k + 1 if mirror else 0)
    out = []
    for end in range(2):
        inside = at - (128 - REACH + REACH // 2 - 1 - k if end else 0)
        used = (k < REACH // 2) & (inside >= 0) & (inside < count)
        index = jnp.clip((window + end) * WINDOW + start + inside, 0, 127)
        out.append(jnp.where(used, picked(line, index), 0.0))
    return jnp.concatenate(out, axis=1)


def ahead(x, d):
    low, high = (turn_lanes(half, -d) for half in x)
    return jnp.where(lanes(low.shape) < 128 - d, low, high), high


def halves(ref, at):
    return ref[at, :128], ref[at, 128:256]


def over_rows(load, count, step, n, unroll=16):
    zeros = (jnp.zeros((8, 128), f32),) * n
    return lax.fori_loop(0, count, lambda k, sums: step(*load(k), sums), zeros, unroll=unroll)


def top_band_of(load, count, top_ref):
    def step(t, sums):
        new = []
        for d in range(0, REACH + 1, 2):
            shifted = ahead(t, d) if d else t
            new += [t[h] * shifted[h] for h in range(2)]
        return tuple(x + y for x, y in zip(sums, new))

    sums = over_rows(lambda k: (load(k),), count, step, 12)
    for h in range(2):
        for j in range(6):
            top_ref[pl.ds(48 * h + 8 * j, 8), :] = sums[2 * j + h]


def band_of(load, count, out_ref, sums_ref, top_ref=None):
    def with_top(t, b, sums):
        new = []
        for d in range(2 if top_ref is not None else 0, REACH + 1, 2):
            shifted = ahead(t, d) if d else t
            if top_ref is None:
                new += [t[h] * shifted[h] for h in range(2)]
            if d:
                new += [b[h] * shifted[h] for h in range(2)]
        return tuple(x + y for x, y in zip(sums, new))

    def with_bottom(t, b, sums, low=0):
        new = []
        for d in range(low, low + 5, 2):
            shifted = ahead(b, d) if d else b
            for left in (b, t):
                new += [left[h] * shifted[h] for h in range(2)]
        return tuple(x + y for x, y in zip(sums, new))

    def at_ends(t, b, sums):
        left, right = ends(t, b)
        new = [left * turn_lanes(right, -d) for d in range(1, REACH, 2)]
        return tuple(x + y for x, y in zip(sums, new))

    def keep(line, value):
        sums_ref[pl.ds(8 * line, 8), :] = value

    if top_ref is not None:
        sums = over_rows(load, count, with_top, 10)
        for h in range(2):
            sums_ref[pl.ds(8 * 24 * h, 48), :] = top_ref[pl.ds(48 * h, 48), :]
            for j in range(1, 6):
                keep(24 * h + 17 + j, sums[2 * j - 2 + h])
    else:
        sums = over_rows(load, count, with_top, 22)
        for h in range(2):
            keep(24 * h, sums[h])
            for j in range(1, 6):
                keep(24 * h + j, sums[4 * j - 2 + h])
                keep(24 * h + 17 + j, sums[4 * j + h])
    sums = over_rows(load, count, with_bottom, 12, 32)
    sums += over_rows(load, count, lambda t, b, sums: with_bottom(t, b, sums, 6), 12, 32)
    for h in range(2):
        for j in range(6):
            keep(24 * h + 6 + j, sums[4 * j + h])
            keep(24 * h + 12 + j, sums[4 * j + 2 + h])
    sums = over_rows(load, count, at_ends, 5)
    for j in range(5):
        keep(LINES + j, sums[j])
    for line in (WIDE, LINES - 1, LINES + 5, LINES + 6, LINES + 7):
        keep(line, jnp.zeros((8, 128), f32))
    parts = [sums_ref[pl.ds(k, LINES + 8, stride=8), :] for k in range(8)]
    while len(parts) > 1:
        parts = [x + y for x, y in zip(parts[::2], parts[1::2])]
    odd = packed_odd(parts[0][LINES:])
    for k in range(out_ref.shape[0]):
        out_ref[k] = parts[0][:LINES]
        out_ref[k, WIDE : WIDE + 1, :] = odd


def along_columns(x):
    shifted = jnp.broadcast_to(turn_lanes(x, -MID), (DIAGS, HALF))
    return pltpu.roll(shifted, 0, axis=1, stride=1, stride_axis=0)


def angles_of(parts_ref, x_ref):
    band = parts_ref[0]
    for k in range(1, parts_ref.shape[0]):
        band = band + parts_ref[k]
    low, high = band[:24], band[24:]
    blank = jnp.zeros((1, HALF), f32)
    for block in range(4):
        for line in (0, 1, DIAGS - 1):
            x_ref[block, line : line + 1, :] = blank
    TT, TB, BT, BB = 0, 1, 2, 3

    def put(block, other, d, value):
        x_ref[block, MID - d : MID - d + 1, :] = value
        x_ref[other, MID + d : MID + d + 1, :] = turn_lanes(value, d)

    def line(k):
        return jnp.concatenate([low[k : k + 1], high[k : k + 1]], axis=1)

    for j in range(6):
        put(TT, TT, 2 * j, line(j))
        put(BB, BB, 2 * j, line(6 + j))
        put(TB, BT, 2 * j, line(12 + j))
        if j:
            put(BT, TB, 2 * j, line(17 + j))
    for window, (block, other) in enumerate(((TT, TT), (BB, BB), (TB, BT), (BT, TB))):
        there = unpacked_odd(low[WIDE : WIDE + 1], 2 * window, False)
        mirror = unpacked_odd(low[WIDE : WIDE + 1], 2 * window, True)
        for j in range(5):
            d = 2 * j + 1
            x_ref[block, MID - d : MID - d + 1, :] = there[j : j + 1]
            x_ref[other, MID + d : MID + d + 1, :] = mirror[j : j + 1]

    tt, tb, bt, bb = (x_ref[k] for k in range(4))
    shape = (DIAGS, HALF)
    i = lanes(shape)
    j = i + MID - lax.broadcasted_iota(jnp.int32, shape, 0)
    i_none, i_one, i_last = i == 0, i == 1, i == HALF - 1
    j_none, j_one, j_last = j == 0, j == 1, j == HALF - 1
    one = lanes((1, HALF))
    one_none, one_one, one_last = one == 0, one == 1, one == HALF - 1

    def less(x, by=1):
        return turn_lines(x, -by)

    def more(x, by=1):
        return turn_lines(x, by)

    def up(x):
        return turn_lanes(x, 1)

    def down(x):
        return turn_lanes(x, -1)

    def both_sides(blocks, c_row, s_row, c_col, s_col):
        tt, tb, bt, bb = blocks
        tt, tb = c_col * tt - s_col * tb, s_col * tt + c_col * tb
        bt, bb = c_col * bt - s_col * bb, s_col * bt + c_col * bb
        tt, bt = c_row * tt - s_row * bt, s_row * tt + c_row * bt
        tb, bb = c_row * tb - s_row * bb, s_row * tb + c_row * bb
        return tt, tb, bt, bb

    cosines, sines = [], []
    blocks = tt, tb, bt, bb
    first, second, coupling = (x[MID : MID + 1] for x in (tt, bb, tb))
    for turn in range(ROUNDS):
        difference = second - first
        direction = jnp.where(difference >= 0, 1.0, -1.0)
        denominator = (
            jnp.abs(difference)
            + jnp.sqrt(difference * difference + 4.0 * coupling * coupling)
            + 1e-06 * (first + second)
        )
        tangent = direction * 2.0 * coupling / denominator
        c = lax.rsqrt(1.0 + tangent * tangent)
        s = tangent * c
        cosines.append(c)
        sines.append(s)
        if turn == ROUNDS - 1:
            break
        here = both_sides([x[MID : MID + 1] for x in blocks], c, s, c, s)
        next_one = both_sides([x[MID - 1 : MID] for x in blocks], c, s, down(c), down(s))
        next_two = both_sides([x[MID - 2 : MID - 1] for x in blocks], c, s, turn_lanes(c, -2), turn_lanes(s, -2))
        first = jnp.where(one_none, here[0], jnp.where(one_one, up(here[3]), up(here[0])))
        second = jnp.where(one_last, here[0], down(here[3]))
        coupling = jnp.where(
            one_none,
            next_one[1],
            jnp.where(one_one, up(next_two[3]), jnp.where(one_last, up(next_one[0]), up(next_two[1]))),
        )
        if turn == ROUNDS - 2:
            continue
        tt, tb, bt, bb = both_sides(
            blocks,
            jnp.broadcast_to(c, shape),
            jnp.broadcast_to(s, shape),
            along_columns(c),
            along_columns(s),
        )
        column, corner = jnp.where(j_none, tb, tt), jnp.where(j_none, bb, bt)
        blocks = (
            jnp.where(
                i_none,
                jnp.where(j_none, tt, less(column)),
                jnp.where(j_none, up(more(jnp.where(i_none, bt, tt))), up(jnp.where(i_none, corner, column))),
            ),
            jnp.where(
                i_none,
                more(tb),
                jnp.where(j_last, up(more(tt)), up(more(jnp.where(i_none, bb, tb), 2))),
            ),
            jnp.where(
                i_last,
                less(tt),
                jnp.where(
                    j_none, down(less(bt)), jnp.where(j_one, down(less(bb, 2)), down(less(bt, 2)))
                ),
            ),
            jnp.where(
                i_last,
                jnp.where(j_last, tt, more(tb)),
                jnp.where(j_last, down(less(bt)), down(bb)),
            ),
        )
    return cosines, sines


def advanced(t, b):
    at = lanes(t[0].shape)
    t0, t1, b0, b1 = turn_lanes(t[0], 1), turn_lanes(t[1], 1), turn_lanes(b[0], -1), turn_lanes(b[1], -1)
    return (
        (
            jnp.where(at >= 2, t0, jnp.where(at == 1, turn_lanes(b[0], 1), t[0])),
            jnp.where(at >= 1, t1, t0),
        ),
        (jnp.where(at == 127, b1, b0), jnp.where(at == 127, t[1], b1)),
    )


MOVES = ROUNDS - 1


def retreated_top(t, b):
    at = lanes(t[0].shape)
    back = [turn_lanes(x, -MOVES) for x in t]
    from_bottom = picked(b[1], (250 - at) % 128)
    return (
        jnp.where(at == 0, t[0], jnp.where(at < 128 - MOVES, back[0], back[1])),
        jnp.where(at < 128 - MOVES, back[1], from_bottom),
    )


def retreated_bottom(t, b):
    at = lanes(t[0].shape)
    on = [turn_lanes(x, MOVES) for x in b]
    from_top = picked(t[0], (MOVES - at) % 128)
    return (
        jnp.where(at < MOVES, from_top, on[0]),
        jnp.where(at < MOVES, on[0], on[1]),
    )


def unfolded_bottom(t, b):
    at = lanes(t[0].shape)
    index = (122 - at) % 128
    low, high = picked(b[0], index), picked(b[1], index)
    return (
        jnp.where(at <= 122, high, low),
        jnp.where(at <= 122, low, turn_lanes(t[0], 122)),
    )


def turned_chunks(load, store, count, rows, cosines, sines):
    def chunk(k, carry):
        t, b = load(k)
        for turn in range(ROUNDS):
            c, s = cosines[turn], sines[turn]
            t, b = (
                tuple(c[h] * t[h] - s[h] * b[h] for h in range(2)),
                tuple(s[h] * t[h] + c[h] * b[h] for h in range(2)),
            )
            if turn < MOVES:
                t, b = advanced(t, b)
        store(k, t, b)
        return carry

    def wide(x):
        x = jnp.broadcast_to(x, (rows, HALF))
        return x[:, :128], x[:, 128:]

    cosines, sines = [wide(c) for c in cosines], [wide(s) for s in sines]
    lax.fori_loop(0, count, chunk, 0)


def rows_at(k, rows):
    return pl.ds(pl.multiple_of(k * rows, rows), rows)


CHUNK = 256


def first_band(p_ref, out_ref, b_ref, sums_ref):
    def fold(k, carry):
        at = rows_at(k, CHUNK)
        b_ref[at, :128], b_ref[at, 128:] = mirrored(p_ref[at, 256:384], p_ref[at, 384:])
        return carry

    lax.fori_loop(0, p_ref.shape[0] // CHUNK, fold, 0)

    def load(k):
        at = rows_at(k, 8)
        return halves(p_ref, at), halves(b_ref, at)

    band_of(load, p_ref.shape[0] // 8, out_ref, sums_ref)


def first_angles(parts_ref, turns_ref, x_ref):
    cosines, sines = angles_of(parts_ref, x_ref)
    turns_ref[...] = jnp.zeros_like(turns_ref)
    for k in range(ROUNDS):
        turns_ref[k : k + 1, :] = cosines[k]
        turns_ref[8 + k : 9 + k, :] = sines[k]


def given(turns_ref):
    return (
        [turns_ref[k : k + 1, :] for k in range(ROUNDS)],
        [turns_ref[8 + k : 9 + k, :] for k in range(ROUNDS)],
    )


def own_turn(turns_ref, p_ref, b_ref, t_out, top_ref):
    def load(k):
        at = rows_at(k, CHUNK)
        return halves(p_ref, at), halves(b_ref, at)

    def store(k, t, b):
        at = rows_at(k, CHUNK)
        t_out[at, :128], t_out[at, 128:] = retreated_top(t, b)

    turned_chunks(load, store, t_out.shape[0] // CHUNK, CHUNK, *given(turns_ref))
    top_band_of(lambda k: halves(t_out, rows_at(k, 8)), t_out.shape[0] // 8, top_ref)


def arrived_turn(turns_ref, p_ref, t_ref, top_ref, b_out, out_ref, sums_ref):
    def load(k):
        at = rows_at(k, CHUNK)
        return halves(p_ref, at), mirrored(p_ref[at, 256:384], p_ref[at, 384:])

    def store(k, t, b):
        at = rows_at(k, CHUNK)
        b_out[at, :128], b_out[at, 128:] = retreated_bottom(t, b)

    turned_chunks(load, store, t_ref.shape[0] // CHUNK, CHUNK, *given(turns_ref))

    def rows(k):
        at = rows_at(k, 8)
        return halves(t_ref, at), halves(b_out, at)

    band_of(rows, t_ref.shape[0] // 8, out_ref, sums_ref, top_ref)


def second_turn(parts_ref, t_ref, b_ref, out_ref, x_ref):
    cosines, sines = angles_of(parts_ref, x_ref)

    def load(k):
        at = rows_at(k, CHUNK)
        return halves(t_ref, at), halves(b_ref, at)

    def store(k, t, b):
        at = rows_at(k, CHUNK)
        out_ref[at, :128], out_ref[at, 128:256] = retreated_top(t, b)
        out_ref[at, 256:384], out_ref[at, 384:] = unfolded_bottom(t, b)

    turned_chunks(load, store, t_ref.shape[0] // CHUNK, CHUNK, cosines, sines)


def call(body, outs, args, scratch=()):
    vmem = pl.BlockSpec(memory_space=pltpu.VMEM)
    shapes = [jax.ShapeDtypeStruct(s, f32) for s in outs]
    return pl.pallas_call(
        body,
        out_shape=shapes,
        in_specs=[vmem] * len(args),
        out_specs=[vmem] * len(outs),
        scratch_shapes=[pltpu.VMEM(s, f32) for s in scratch],
        compiler_params=pltpu.CompilerParams(vmem_limit_bytes=32 * 1024 * 1024),
        interpret=INTERPRET,
    )(*args)


ROW_AXES = ("z3", "z2", "z1", "z0", "side")
FIRST_SUM = (("z1", "z0", "side"), ("z3", "z2"))
SECOND_SUM = (("z0", "side"), ("z3", "z2", "z1"))


def exchanged(parts, stages):
    near, far = stages
    arrived = lax.all_to_all(parts, near, 0, 0, tiled=True)
    total = arrived[0]
    for k in range(1, arrived.shape[0]):
        total = total + arrived[k]
    again = jnp.broadcast_to(total[None], (lax.axis_size(far), *total.shape))
    return lax.all_to_all(again, far, 0, 0, tiled=True)


SUMS = [(8 * LINES + 64, 128)]
STATE = [(4, DIAGS, HALF)]


TOP = (2 * 6 * 8, 128)
TURNS = (16, HALF)


def per_device(snapshots):
    rows = snapshots.shape[0]
    square = (rows, HALF)
    first, second = ((lax.axis_size(stages[0]), LINES, 128) for stages in (FIRST_SUM, SECOND_SUM))
    groups = lax.axis_size("grp")
    onward = [(i, (i + 1) % groups) for i in range(groups)]
    raw = lax.ppermute(snapshots, "grp", onward)
    parts, b = call(first_band, [first, square], [snapshots], SUMS)
    (turns,) = call(first_angles, [TURNS], [exchanged(parts, FIRST_SUM)], STATE)
    their_turns = lax.ppermute(turns, "grp", onward)
    t, top = call(own_turn, [square, TOP], [turns, snapshots, b])
    b, parts = call(arrived_turn, [square, second], [their_turns, raw, t, top], SUMS)
    (out,) = call(second_turn, [(rows, 2 * HALF)], [exchanged(parts, SECOND_SUM), t, b], STATE)
    return out


def solution(mesh):
    sizes = (mesh.shape["grp"], mesh.shape["row"] // 16, 2, 2, 2, 2)
    fine = Mesh(mesh.devices.reshape(sizes), ("grp", *ROW_AXES))
    placed = P(ROW_AXES, "grp")
    return jax.shard_map(per_device, mesh=fine, in_specs=(placed,), out_specs=placed, check_vma=False)
```

```python
import jax
import jax.numpy as jnp
from jax import lax
from jax.experimental import pallas as pl
from jax.experimental.pallas import tpu as pltpu
from jax.sharding import Mesh
from jax.sharding import PartitionSpec as P

ROUNDS = 6
HALF = 256
REACH = 10
DIAGS = 24
MID = 12
WIDE = 23
LINES = 48
WINDOW = 16

f32 = jnp.float32
INTERPRET = False


def lanes(shape):
    return lax.broadcasted_iota(jnp.int32, shape, 1)


def turn_lanes(x, by):
    by %= x.shape[1]
    return pltpu.roll(x, by, axis=1) if by else x


def turn_lines(x, by):
    return pltpu.roll(x, by % x.shape[0], axis=0)


def picked(x, index):
    return jnp.take_along_axis(x, index, axis=1, mode="promise_in_bounds")


def mirrored(low, high):
    index = 127 - lanes(low.shape)
    return picked(high, index), picked(low, index)


def ends(t, b):
    at = lanes(t[0].shape)
    e = jnp.where(
        at < 16,
        t[0],
        jnp.where(at < 32, turn_lanes(t[1], 26), jnp.where(at < 48, turn_lanes(b[0], 32), turn_lanes(b[1], 58))),
    )
    swapped = jnp.where(at < 96, turn_lanes(e, 32), turn_lanes(e, 96))
    return jnp.where(at < 64, e, turn_lanes(e, 64)), jnp.where(at < 64, e, swapped)


def place_of_odd(shape):
    k = lax.broadcasted_iota(jnp.int32, shape, 0)
    return k, REACH // 2 - k, (k * (REACH + 1 - k)) // 2


def packed_odd(sums):
    k, count, start = place_of_odd(sums.shape)
    at = lanes(sums.shape)
    inside = at % WINDOW - start
    first = jnp.where((at // WINDOW) % 2 == 0, 0, REACH // 2 - 1 - k)
    index = jnp.clip(at - at % WINDOW + first + inside, 0, 127)
    used = (k < REACH // 2) & (inside >= 0) & (inside < count)
    return jnp.sum(jnp.where(used, picked(sums, index), 0.0), axis=0, keepdims=True)


def unpacked_odd(line, window, mirror):
    line = jnp.broadcast_to(line, (8, 128))
    k, count, start = place_of_odd(line.shape)
    at = lanes(line.shape) - (2 * k + 1 if mirror else 0)
    out = []
    for end in range(2):
        inside = at - (128 - REACH + REACH // 2 - 1 - k if end else 0)
        used = (k < REACH // 2) & (inside >= 0) & (inside < count)
        index = jnp.clip((window + end) * WINDOW + start + inside, 0, 127)
        out.append(jnp.where(used, picked(line, index), 0.0))
    return jnp.concatenate(out, axis=1)


def ahead(x, d):
    low, high = (turn_lanes(half, -d) for half in x)
    return jnp.where(lanes(low.shape) < 128 - d, low, high), high


def halves(ref, at):
    return ref[at, :128], ref[at, 128:256]


def over_rows(load, count, step, n, unroll=16):
    zeros = (jnp.zeros((8, 128), f32),) * n
    return lax.fori_loop(0, count, lambda k, sums: step(*load(k), sums), zeros, unroll=unroll)


def top_band_of(load, count, top_ref):
    def step(t, sums):
        new = []
        for d in range(0, REACH + 1, 2):
            shifted = ahead(t, d) if d else t
            new += [t[h] * shifted[h] for h in range(2)]
        return tuple(x + y for x, y in zip(sums, new))

    sums = over_rows(lambda k: (load(k),), count, step, 12)
    for h in range(2):
        for j in range(6):
            top_ref[pl.ds(48 * h + 8 * j, 8), :] = sums[2 * j + h]


def band_of(load, count, out_ref, sums_ref, top_ref=None):
    def with_top(t, b, sums):
        new = []
        for d in range(2 if top_ref is not None else 0, REACH + 1, 2):
            shifted = ahead(t, d) if d else t
            if top_ref is None:
                new += [t[h] * shifted[h] for h in range(2)]
            if d:
                new += [b[h] * shifted[h] for h in range(2)]
        return tuple(x + y for x, y in zip(sums, new))

    def with_bottom(t, b, sums, low=0):
        new = []
        for d in range(low, low + 5, 2):
            shifted = ahead(b, d) if d else b
            for left in (b, t):
                new += [left[h] * shifted[h] for h in range(2)]
        return tuple(x + y for x, y in zip(sums, new))

    def at_ends(t, b, sums):
        left, right = ends(t, b)
        new = [left * turn_lanes(right, -d) for d in range(1, REACH, 2)]
        return tuple(x + y for x, y in zip(sums, new))

    def keep(line, value):
        sums_ref[pl.ds(8 * line, 8), :] = value

    if top_ref is not None:
        sums = over_rows(load, count, with_top, 10, 32)
        for h in range(2):
            sums_ref[pl.ds(8 * 24 * h, 48), :] = top_ref[pl.ds(48 * h, 48), :]
            for j in range(1, 6):
                keep(24 * h + 17 + j, sums[2 * j - 2 + h])
    else:
        sums = over_rows(load, count, with_top, 22)
        for h in range(2):
            keep(24 * h, sums[h])
            for j in range(1, 6):
                keep(24 * h + j, sums[4 * j - 2 + h])
                keep(24 * h + 17 + j, sums[4 * j + h])
    sums = over_rows(load, count, with_bottom, 12, 32)
    sums += over_rows(load, count, lambda t, b, sums: with_bottom(t, b, sums, 6), 12, 32)
    for h in range(2):
        for j in range(6):
            keep(24 * h + 6 + j, sums[4 * j + h])
            keep(24 * h + 12 + j, sums[4 * j + 2 + h])
    sums = over_rows(load, count, at_ends, 5)
    for j in range(5):
        keep(LINES + j, sums[j])
    for line in (WIDE, LINES - 1, LINES + 5, LINES + 6, LINES + 7):
        keep(line, jnp.zeros((8, 128), f32))
    parts = [sums_ref[pl.ds(k, LINES + 8, stride=8), :] for k in range(8)]
    while len(parts) > 1:
        parts = [x + y for x, y in zip(parts[::2], parts[1::2])]
    odd = packed_odd(parts[0][LINES:])
    for k in range(out_ref.shape[0]):
        out_ref[k] = parts[0][:LINES]
        out_ref[k, WIDE : WIDE + 1, :] = odd


def along_columns(x):
    shifted = jnp.broadcast_to(turn_lanes(x, -MID), (DIAGS, HALF))
    return pltpu.roll(shifted, 0, axis=1, stride=1, stride_axis=0)


def angles_of(parts_ref, x_ref):
    band = parts_ref[0]
    for k in range(1, parts_ref.shape[0]):
        band = band + parts_ref[k]
    low, high = band[:24], band[24:]
    blank = jnp.zeros((1, HALF), f32)
    for block in range(4):
        for line in (0, 1, DIAGS - 1):
            x_ref[block, line : line + 1, :] = blank
    TT, TB, BT, BB = 0, 1, 2, 3

    def put(block, other, d, value):
        x_ref[block, MID - d : MID - d + 1, :] = value
        x_ref[other, MID + d : MID + d + 1, :] = turn_lanes(value, d)

    def line(k):
        return jnp.concatenate([low[k : k + 1], high[k : k + 1]], axis=1)

    for j in range(6):
        put(TT, TT, 2 * j, line(j))
        put(BB, BB, 2 * j, line(6 + j))
        put(TB, BT, 2 * j, line(12 + j))
        if j:
            put(BT, TB, 2 * j, line(17 + j))
    for window, (block, other) in enumerate(((TT, TT), (BB, BB), (TB, BT), (BT, TB))):
        there = unpacked_odd(low[WIDE : WIDE + 1], 2 * window, False)
        mirror = unpacked_odd(low[WIDE : WIDE + 1], 2 * window, True)
        for j in range(5):
            d = 2 * j + 1
            x_ref[block, MID - d : MID - d + 1, :] = there[j : j + 1]
            x_ref[other, MID + d : MID + d + 1, :] = mirror[j : j + 1]

    tt, tb, bt, bb = (x_ref[k] for k in range(4))
    shape = (DIAGS, HALF)
    i = lanes(shape)
    j = i + MID - lax.broadcasted_iota(jnp.int32, shape, 0)
    i_none, i_one, i_last = i == 0, i == 1, i == HALF - 1
    j_none, j_one, j_last = j == 0, j == 1, j == HALF - 1
    one = lanes((1, HALF))
    one_none, one_one, one_last = one == 0, one == 1, one == HALF - 1

    def less(x, by=1):
        return turn_lines(x, -by)

    def more(x, by=1):
        return turn_lines(x, by)

    def up(x):
        return turn_lanes(x, 1)

    def down(x):
        return turn_lanes(x, -1)

    def both_sides(blocks, c_row, s_row, c_col, s_col):
        tt, tb, bt, bb = blocks
        tt, tb = c_col * tt - s_col * tb, s_col * tt + c_col * tb
        bt, bb = c_col * bt - s_col * bb, s_col * bt + c_col * bb
        tt, bt = c_row * tt - s_row * bt, s_row * tt + c_row * bt
        tb, bb = c_row * tb - s_row * bb, s_row * tb + c_row * bb
        return tt, tb, bt, bb

    cosines, sines = [], []
    blocks = tt, tb, bt, bb
    first, second, coupling = (x[MID : MID + 1] for x in (tt, bb, tb))
    for turn in range(ROUNDS):
        difference = second - first
        direction = jnp.where(difference >= 0, 1.0, -1.0)
        denominator = (
            jnp.abs(difference)
            + jnp.sqrt(difference * difference + 4.0 * coupling * coupling)
            + 1e-06 * (first + second)
        )
        tangent = direction * 2.0 * coupling / denominator
        c = lax.rsqrt(1.0 + tangent * tangent)
        s = tangent * c
        cosines.append(c)
        sines.append(s)
        if turn == ROUNDS - 1:
            break
        here = both_sides([x[MID : MID + 1] for x in blocks], c, s, c, s)
        next_one = both_sides([x[MID - 1 : MID] for x in blocks], c, s, down(c), down(s))
        next_two = both_sides([x[MID - 2 : MID - 1] for x in blocks], c, s, turn_lanes(c, -2), turn_lanes(s, -2))
        first = jnp.where(one_none, here[0], jnp.where(one_one, up(here[3]), up(here[0])))
        second = jnp.where(one_last, here[0], down(here[3]))
        coupling = jnp.where(
            one_none,
            next_one[1],
            jnp.where(one_one, up(next_two[3]), jnp.where(one_last, up(next_one[0]), up(next_two[1]))),
        )
        if turn == ROUNDS - 2:
            continue
        tt, tb, bt, bb = both_sides(
            blocks,
            jnp.broadcast_to(c, shape),
            jnp.broadcast_to(s, shape),
            along_columns(c),
            along_columns(s),
        )
        column, corner = jnp.where(j_none, tb, tt), jnp.where(j_none, bb, bt)
        blocks = (
            jnp.where(
                i_none,
                jnp.where(j_none, tt, less(column)),
                jnp.where(j_none, up(more(jnp.where(i_none, bt, tt))), up(jnp.where(i_none, corner, column))),
            ),
            jnp.where(
                i_none,
                more(tb),
                jnp.where(j_last, up(more(tt)), up(more(jnp.where(i_none, bb, tb), 2))),
            ),
            jnp.where(
                i_last,
                less(tt),
                jnp.where(
                    j_none, down(less(bt)), jnp.where(j_one, down(less(bb, 2)), down(less(bt, 2)))
                ),
            ),
            jnp.where(
                i_last,
                jnp.where(j_last, tt, more(tb)),
                jnp.where(j_last, down(less(bt)), down(bb)),
            ),
        )
    return cosines, sines


def advanced(t, b):
    at = lanes(t[0].shape)
    t0, t1, b0, b1 = turn_lanes(t[0], 1), turn_lanes(t[1], 1), turn_lanes(b[0], -1), turn_lanes(b[1], -1)
    return (
        (
            jnp.where(at >= 2, t0, jnp.where(at == 1, turn_lanes(b[0], 1), t[0])),
            jnp.where(at >= 1, t1, t0),
        ),
        (jnp.where(at == 127, b1, b0), jnp.where(at == 127, t[1], b1)),
    )


MOVES = ROUNDS - 1


def retreated_top(t, b):
    at = lanes(t[0].shape)
    back = [turn_lanes(x, -MOVES) for x in t]
    from_bottom = picked(b[1], (250 - at) % 128)
    return (
        jnp.where(at == 0, t[0], jnp.where(at < 128 - MOVES, back[0], back[1])),
        jnp.where(at < 128 - MOVES, back[1], from_bottom),
    )


def retreated_bottom(t, b):
    at = lanes(t[0].shape)
    on = [turn_lanes(x, MOVES) for x in b]
    from_top = picked(t[0], (MOVES - at) % 128)
    return (
        jnp.where(at < MOVES, from_top, on[0]),
        jnp.where(at < MOVES, on[0], on[1]),
    )


def unfolded_bottom(t, b):
    at = lanes(t[0].shape)
    index = (122 - at) % 128
    low, high = picked(b[0], index), picked(b[1], index)
    return (
        jnp.where(at <= 122, high, low),
        jnp.where(at <= 122, low, turn_lanes(t[0], 122)),
    )


def turned_chunks(load, store, count, rows, cosines, sines):
    def chunk(k, carry):
        t, b = load(k)
        for turn in range(ROUNDS):
            c, s = cosines[turn], sines[turn]
            t, b = (
                tuple(c[h] * t[h] - s[h] * b[h] for h in range(2)),
                tuple(s[h] * t[h] + c[h] * b[h] for h in range(2)),
            )
            if turn < MOVES:
                t, b = advanced(t, b)
        store(k, t, b)
        return carry

    def wide(x):
        x = jnp.broadcast_to(x, (rows, HALF))
        return x[:, :128], x[:, 128:]

    cosines, sines = [wide(c) for c in cosines], [wide(s) for s in sines]
    lax.fori_loop(0, count, chunk, 0)


def rows_at(k, rows):
    return pl.ds(pl.multiple_of(k * rows, rows), rows)


CHUNK = 256


def first_band(p_ref, out_ref, b_ref, sums_ref):
    def fold(k, carry):
        at = rows_at(k, CHUNK)
        b_ref[at, :128], b_ref[at, 128:] = mirrored(p_ref[at, 256:384], p_ref[at, 384:])
        return carry

    lax.fori_loop(0, p_ref.shape[0] // CHUNK, fold, 0)

    def load(k):
        at = rows_at(k, 8)
        return halves(p_ref, at), halves(b_ref, at)

    band_of(load, p_ref.shape[0] // 8, out_ref, sums_ref)


def first_angles(parts_ref, turns_ref, x_ref):
    cosines, sines = angles_of(parts_ref, x_ref)
    turns_ref[...] = jnp.zeros_like(turns_ref)
    for k in range(ROUNDS):
        turns_ref[k : k + 1, :] = cosines[k]
        turns_ref[8 + k : 9 + k, :] = sines[k]


def given(turns_ref):
    return (
        [turns_ref[k : k + 1, :] for k in range(ROUNDS)],
        [turns_ref[8 + k : 9 + k, :] for k in range(ROUNDS)],
    )


def own_turn(turns_ref, p_ref, b_ref, t_out, top_ref):
    def load(k):
        at = rows_at(k, CHUNK)
        return halves(p_ref, at), halves(b_ref, at)

    def store(k, t, b):
        at = rows_at(k, CHUNK)
        t_out[at, :128], t_out[at, 128:] = retreated_top(t, b)

    turned_chunks(load, store, t_out.shape[0] // CHUNK, CHUNK, *given(turns_ref))
    top_band_of(lambda k: halves(t_out, rows_at(k, 8)), t_out.shape[0] // 8, top_ref)


def arrived_turn(turns_ref, p_ref, t_ref, top_ref, b_out, out_ref, sums_ref):
    def load(k):
        at = rows_at(k, CHUNK)
        return halves(p_ref, at), mirrored(p_ref[at, 256:384], p_ref[at, 384:])

    def store(k, t, b):
        at = rows_at(k, CHUNK)
        b_out[at, :128], b_out[at, 128:] = retreated_bottom(t, b)

    turned_chunks(load, store, t_ref.shape[0] // CHUNK, CHUNK, *given(turns_ref))

    def rows(k):
        at = rows_at(k, 8)
        return halves(t_ref, at), halves(b_out, at)

    band_of(rows, t_ref.shape[0] // 8, out_ref, sums_ref, top_ref)


def second_turn(parts_ref, t_ref, b_ref, out_ref, x_ref):
    cosines, sines = angles_of(parts_ref, x_ref)

    def load(k):
        at = rows_at(k, CHUNK)
        return halves(t_ref, at), halves(b_ref, at)

    def store(k, t, b):
        at = rows_at(k, CHUNK)
        out_ref[at, :128], out_ref[at, 128:256] = retreated_top(t, b)
        out_ref[at, 256:384], out_ref[at, 384:] = unfolded_bottom(t, b)

    turned_chunks(load, store, t_ref.shape[0] // CHUNK, CHUNK, cosines, sines)


def call(body, outs, args, scratch=()):
    vmem = pl.BlockSpec(memory_space=pltpu.VMEM)
    shapes = [jax.ShapeDtypeStruct(s, f32) for s in outs]
    return pl.pallas_call(
        body,
        out_shape=shapes,
        in_specs=[vmem] * len(args),
        out_specs=[vmem] * len(outs),
        scratch_shapes=[pltpu.VMEM(s, f32) for s in scratch],
        compiler_params=pltpu.CompilerParams(vmem_limit_bytes=32 * 1024 * 1024),
        interpret=INTERPRET,
    )(*args)


ROW_AXES = ("z3", "z2", "z1", "z0", "side")
FIRST_SUM = (("z1", "z0", "side"), ("z3", "z2"))
SECOND_SUM = (("z0", "side"), ("z3", "z2", "z1"))


def exchanged(parts, stages):
    near, far = stages
    arrived = lax.all_to_all(parts, near, 0, 0, tiled=True)
    total = arrived[0]
    for k in range(1, arrived.shape[0]):
        total = total + arrived[k]
    again = jnp.broadcast_to(total[None], (lax.axis_size(far), *total.shape))
    return lax.all_to_all(again, far, 0, 0, tiled=True)


SUMS = [(8 * LINES + 64, 128)]
STATE = [(4, DIAGS, HALF)]


TOP = (2 * 6 * 8, 128)
TURNS = (16, HALF)


def per_device(snapshots):
    rows = snapshots.shape[0]
    square = (rows, HALF)
    first, second = ((lax.axis_size(stages[0]), LINES, 128) for stages in (FIRST_SUM, SECOND_SUM))
    groups = lax.axis_size("grp")
    onward = [(i, (i + 1) % groups) for i in range(groups)]
    raw = lax.ppermute(snapshots, "grp", onward)
    parts, b = call(first_band, [first, square], [snapshots], SUMS)
    (turns,) = call(first_angles, [TURNS], [exchanged(parts, FIRST_SUM)], STATE)
    their_turns = lax.ppermute(turns, "grp", onward)
    t, top = call(own_turn, [square, TOP], [turns, snapshots, b])
    b, parts = call(arrived_turn, [square, second], [their_turns, raw, t, top], SUMS)
    (out,) = call(second_turn, [(rows, 2 * HALF)], [exchanged(parts, SECOND_SUM), t, b], STATE)
    return out


def solution(mesh):
    sizes = (mesh.shape["grp"], mesh.shape["row"] // 16, 2, 2, 2, 2)
    fine = Mesh(mesh.devices.reshape(sizes), ("grp", *ROW_AXES))
    placed = P(ROW_AXES, "grp")
    return jax.shard_map(per_device, mesh=fine, in_specs=(placed,), out_specs=placed, check_vma=False)
```
